768 devices in a mesh: dp: 384 (over x_hi, z, y, core), opt: 2 (over x_lo).
Axes of the slice: x: 4 (x_hi: 2, x_lo: 2; x = x_hi * 2 + x_lo), y: 8, z: 12, core: 2. Of those that a mesh axis runs over, the one named last changes fastest.
Arguments:
- img_resid: bfloat16 [98304, 1152], P(('dp', 'opt')), may hold values from -6 to 6
- img_hidden: bfloat16 [98304, 1024], P(('dp', 'opt')), may hold values from -6 to 6
- txt_resid: bfloat16 [98304, 1152], P('dp'), may hold values from -6 to 6
- txt_hidden: bfloat16 [98304, 1024], P('dp'), may hold values from -6 to 6
- edge_weight: bfloat16 [2, 1024, 128], replicated, may hold values from -0.1875 to 0.1875
- left_root: float32 [2, 1024, 1024], P('opt'), may hold values from -0.125 to 2
- right_root: float32 [2, 128, 128], P('opt'), may hold values from -0.35355339 to 2
- graft_acc: float32 [2, 1024, 128], P('opt'), may hold values from 1e-07 to 100
Outputs:
- updates: float32 [2, 1024, 128], P('opt')
The draws below stay inside these ranges and needn't reach their ends.
All inputs are finite; a program needn't handle non-finite values.
Results may differ from the reference program's by a relative error of at most 0.0038.
Values may be sent and summed in bfloat16 or wider, within the bound.
A program may use at most 32 MiB of HBM per device.

```python
import jax
import jax.numpy as jnp
from jax import lax

D = 1152
BLK = 1024
WINDOW = 3
EDGE = 128
TXT_DP = 256
BATCH = 98304
N_DP = 384


def root_matrix(key, diag_values, order):
    noise = jnp.clip(jax.random.normal(key, (2, order, order), jnp.float32), -4.0, 4.0)
    symmetric = (noise + jnp.swapaxes(noise, 1, 2)) * (0.5 / order ** 0.5)
    identity = jnp.eye(order, dtype=jnp.float32)
    return symmetric * (1.0 - identity) + diag_values[:, :, None] * identity


def draw_left_root(key, part):
    key = jax.random.fold_in(key, 11)
    first_key, second_key = jax.random.split(key)
    diag_values = jnp.exp(jax.random.uniform(second_key, (2, BLK), jnp.float32, jnp.log(0.5), jnp.log(2.0)))
    return root_matrix(first_key, diag_values, BLK)


def draw_right_root(key, part):
    key = jax.random.fold_in(key, 23)
    first_key, second_key = jax.random.split(key)
    diag_values = jnp.exp(jax.random.uniform(second_key, (2, EDGE), jnp.float32, jnp.log(0.5), jnp.log(2.0)))
    return root_matrix(first_key, diag_values, EDGE)


def draw_graft_acc(key, part):
    key = jax.random.fold_in(key, 37)
    scale_key, entry_key = jax.random.split(key)
    tower_scale = jnp.exp(jax.random.uniform(scale_key, (2, 1, 1), jnp.float32, jnp.log(0.0001), jnp.log(100.0)))
    entries = jnp.exp(jax.random.uniform(entry_key, (2, BLK, EDGE), jnp.float32, jnp.log(0.001), jnp.log(1.0)))
    return entries * tower_scale


def block_scale(own_key, shape, cuts, smallest, high):
    def one(dim, parts):
        draws = jax.random.uniform(jax.random.fold_in(jax.random.fold_in(own_key, 6), dim), (parts,), jnp.float32, smallest / len(cuts), high / len(cuts))
        return jnp.repeat(jnp.exp(draws), shape[dim] // parts).reshape((-1,) + (1,) * (len(shape) - dim - 1))

    gain = one(*cuts[0])
    for cut in cuts[1:]:
        gain = gain * one(*cut)
    return gain


def normal_values(key, extent, spread, reach, shards=(), kind=jnp.bfloat16):
    values = spread * jax.random.normal(key, extent, jnp.float32)
    if shards:
        values = values * block_scale(key, extent, shards, -0.22, 0.18)
    return jnp.clip(values, -reach, reach).astype(kind)


def setup_inputs(seed: int = 0) -> dict:
    arg_keys = jax.random.split(jax.random.key(seed), 9)
    return {
        "img_resid": normal_values(arg_keys[0], (BATCH, D), 1.0, 6.0, ((0, 768),)),
        "img_hidden": normal_values(arg_keys[1], (BATCH, BLK), 1.0, 6.0, ((0, 768),)),
        "txt_resid": normal_values(arg_keys[2], (BATCH, D), 1.0, 6.0, ((0, 384),)),
        "txt_hidden": normal_values(arg_keys[3], (BATCH, BLK), 1.0, 6.0, ((0, 384),)),
        "edge_weight": normal_values(arg_keys[4], (2, BLK, EDGE), BLK ** -0.5, 0.1875),
        "left_root": draw_left_root(jax.random.fold_in(arg_keys[8], 71), 0),
        "right_root": draw_right_root(jax.random.fold_in(arg_keys[8], 71), 0),
        "graft_acc": draw_graft_acc(jax.random.fold_in(arg_keys[8], 71), 0),
    }


def embed_rows(resid, hidden, weight):
    edge_part = jnp.dot(hidden, weight, preferred_element_type=jnp.float32)
    stream = resid.astype(jnp.float32)
    stream = jnp.concatenate([stream[:, :BLK], stream[:, BLK:] + edge_part], axis=1)
    length = jnp.sqrt(lax.optimization_barrier(jnp.sum(stream * stream, axis=1, keepdims=True)) + 1e-06)
    return (stream / length, length)

def back_norm(direction, length, grads):
    radial = lax.optimization_barrier(jnp.sum(direction * grads, axis=1, keepdims=True))
    return ((grads - direction * radial) / length)[:, BLK:].astype(jnp.bfloat16)

def precondition(block_grad, left_mat, right_mat, accum):
    highest = lax.Precision.HIGHEST
    conditioned = jnp.dot(jnp.dot(left_mat, block_grad, precision=highest), right_mat, precision=highest)
    grafted = block_grad / jnp.sqrt(accum + block_grad * block_grad)
    factor = jnp.sqrt(jnp.sum(grafted * grafted)) / jnp.sqrt(jnp.sum(conditioned * conditioned) + 1e-06)
    return conditioned * factor

def reference(img_resid, img_hidden, txt_resid, txt_hidden, edge_weight, left_root, right_root, graft_acc):
    img_dir, img_len = embed_rows(img_resid, img_hidden, edge_weight[0])
    txt_dir, txt_len = embed_rows(txt_resid, txt_hidden, edge_weight[1])
    img_emb = img_dir.astype(jnp.bfloat16)
    txt_emb = txt_dir.astype(jnp.bfloat16)
    img_blocks = img_emb.reshape(N_DP, TXT_DP, D).astype(jnp.float32)
    txt_blocks = txt_emb.reshape(N_DP, TXT_DP, D).astype(jnp.float32)
    eye_block = (lax.broadcasted_iota(jnp.int32, (TXT_DP, TXT_DP), 0) == lax.broadcasted_iota(jnp.int32, (TXT_DP, TXT_DP), 1)).astype(jnp.float32)
    img_grad = jnp.zeros((N_DP, TXT_DP, D), jnp.float32)
    txt_grad = jnp.zeros((N_DP, TXT_DP, D), jnp.float32)
    for offset in range(WINDOW):
        rolled = jnp.roll(txt_blocks, offset, axis=0)
        logits = 10.0 * jnp.einsum('bid,bjd->bij', img_blocks, rolled) - 2.0
        weights = jax.nn.sigmoid(logits)
        if offset == 0:
            weights = weights - eye_block[None]
        weights = weights.astype(jnp.bfloat16).astype(jnp.float32)
        img_grad = img_grad + jnp.einsum('bij,bjd->bid', weights, rolled)
        back = jnp.einsum('bij,bid->bjd', weights, img_blocks)
        txt_grad = txt_grad + jnp.roll(back, -offset, axis=0)
    img_dz = back_norm(img_dir, img_len, img_grad.reshape(BATCH, D))
    txt_dz = back_norm(txt_dir, txt_len, txt_grad.reshape(BATCH, D))
    img_block = jnp.dot(img_hidden.T, img_dz, preferred_element_type=jnp.float32)
    txt_block = jnp.dot(txt_hidden.T, txt_dz, preferred_element_type=jnp.float32)
    img_update = precondition(img_block, left_root[0], right_root[0], graft_acc[0])
    txt_update = precondition(txt_block, left_root[1], right_root[1], graft_acc[1])
    return jnp.stack([img_update, txt_update])
```

```python
import functools

import jax
import jax.numpy as jnp
from jax import lax
from jax.experimental import pallas as pl
from jax.experimental.pallas import tpu as pltpu
from jax.sharding import PartitionSpec as P

WINDOW = 3
NX, NY, NZ = 2, 8, 12
MESH = pl.DeviceIdType.MESH
F32 = jnp.float32
BF16 = jnp.bfloat16


def shifted(block, axis, distance):
    devices = range(lax.axis_size(axis))
    route = [((i - distance) % len(devices), i) for i in devices]
    return lax.ppermute(block, axis, route)


def embed_rows(resid, hidden, weight, split_at):
    edge_part = jnp.dot(hidden, weight, preferred_element_type=F32)
    stream = resid.astype(F32)
    stream = jnp.concatenate([stream[:, :split_at], stream[:, split_at:] + edge_part], axis=1)
    length = jnp.sqrt(jnp.sum(stream * stream, axis=1, keepdims=True) + 1e-06)
    return (stream / length, length)


def edge_back(direction, length, edge_grad, radial, split_at):
    return ((edge_grad - direction[:, split_at:] * radial) / length).astype(BF16)


class Place:
    def __init__(self):
        dp = lax.axis_index("dp")
        self.xl = lax.axis_index("opt")
        self.core = lax.rem(dp, 2)
        self.y = lax.rem(lax.div(dp, 2), NY)
        self.z = lax.rem(lax.div(dp, 2 * NY), NZ)
        self.xh = lax.div(dp, 2 * NY * NZ)

    def at(self, xh=None, z=None, y=None, core=None, xl=None):
        xh = self.xh if xh is None else xh
        z = self.z if z is None else z
        y = self.y if y is None else y
        core = self.core if core is None else core
        xl = self.xl if xl is None else xl
        return (((xh * NZ + z) * NY + y) * 2 + core, xl)


def reduce_kernel(
    p_ref, left_hbm, right_ref, acc_ref, out_ref,
    left_ref, cbuf, acc1, xsend, xbuf, acc2, ysend, ybuf, zbuf, gbuf, cond,
    load_sem, csend_sem, crecv_sem, xs_sem, xr_sem, ys_sem, yr_sem, zs_sem, zr_sem,
    gs_sem, gr_sem, hs_sem, hr_sem, ks_sem, kr_sem,
):
    me = Place()
    load = pltpu.make_async_copy(left_hbm, left_ref, load_sem)
    load.start()
    oc = 1 - me.core
    x = me.xh * 2 + me.xl
    xpeer = []
    for k in range(1, 4):
        px = lax.rem(x + k, 4)
        xpeer.append((px, me.at(xh=lax.div(px, 2), xl=lax.rem(px, 2))))
    ypeer = [(lax.rem(me.y + k, NY), me.at(y=lax.rem(me.y + k, NY))) for k in range(1, NY)]
    zpeer = [(lax.rem(me.z + k, NZ), me.at(z=lax.rem(me.z + k, NZ))) for k in range(1, NZ)]
    cpeer = me.at(core=oc)
    hpeer = me.at(xh=1 - me.xh)

    barrier = pltpu.get_barrier_semaphore()
    peers = [cpeer] + [d for _, d in xpeer + ypeer + zpeer]
    for d in peers:
        pl.semaphore_signal(barrier, inc=1, device_id=d, device_id_type=MESH)
    pl.semaphore_wait(barrier, len(peers))

    def remote(src, dst, s, r, d):
        return pltpu.make_async_remote_copy(
            src_ref=src, dst_ref=dst, send_sem=s, recv_sem=r, device_id=d, device_id_type=MESH
        )

    mine = pl.ds(pl.multiple_of(me.core * 512, 512), 512)
    theirs = pl.ds(pl.multiple_of(oc * 512, 512), 512)
    sent = []
    ccopies = []
    for t in range(2):
        c = remote(p_ref.at[t, theirs], cbuf.at[t], csend_sem.at[t], crecv_sem.at[t], cpeer)
        c.start()
        ccopies.append(c)
    for t in range(2):
        ccopies[t].wait_recv()
        acc1[t] = p_ref[t, mine] + cbuf[t]
    sent += ccopies
    xcopies = []
    for k in (2, 1, 3):
        px, d = xpeer[k - 1]
        rows = pl.ds(pl.multiple_of(lax.div(px, 2) * 256, 256), 256)
        xsend[k - 1] = acc1[lax.rem(px, 2), rows].astype(BF16)
        c = remote(xsend.at[k - 1], xbuf.at[k - 1], xs_sem.at[k - 1], xr_sem.at[k - 1], d)
        c.start()
        xcopies.append(c)
    total = acc1[me.xl, pl.ds(pl.multiple_of(me.xh * 256, 256), 256)]
    for c, k in zip(xcopies, (2, 1, 3)):
        c.wait_recv()
    for k in range(3):
        total = total + xbuf[k].astype(F32)
    acc2[...] = total
    sent += xcopies
    ysend[...] = total.astype(BF16)
    ycopies = []
    for k in (4, 3, 5, 2, 6, 1, 7):
        py, d = ypeer[k - 1]
        c = remote(
            ysend.at[pl.ds(pl.multiple_of(py * 32, 32), 32)], ybuf.at[k - 1],
            ys_sem.at[k - 1], yr_sem.at[k - 1], d,
        )
        c.start()
        ycopies.append(c)
    part = acc2[pl.ds(pl.multiple_of(me.y * 32, 32), 32)]
    for c in ycopies:
        c.wait_recv()
    for k in range(NY - 1):
        part = part + ybuf[k].astype(F32)
    sent += ycopies
    zbuf[me.z] = part.astype(BF16)
    zcopies = []
    for k in (6, 5, 7, 4, 8, 3, 9, 2, 10, 1, 11):
        pz, d = zpeer[k - 1]
        c = remote(zbuf.at[me.z], zbuf.at[me.z], zs_sem.at[k - 1], zr_sem.at[k - 1], d)
        c.start()
        zcopies.append((k, c))
    for k, c in zcopies:
        src = lax.rem(me.z + NZ - k, NZ)
        remote(zbuf.at[src], zbuf.at[src], zs_sem.at[k - 1], zr_sem.at[k - 1], cpeer).wait_recv()
        sent.append(c)
    part = zbuf[0].astype(F32)
    for k in range(1, NZ):
        part = part + zbuf[k].astype(F32)
    base = me.core * 512 + me.xh * 256
    own = pl.ds(pl.multiple_of(base + me.y * 32, 32), 32)
    gbuf[own] = part
    gcopies = []
    for k in (4, 3, 5, 2, 6, 1, 7):
        py, d = ypeer[k - 1]
        c = remote(gbuf.at[own], gbuf.at[own], gs_sem.at[k - 1], gr_sem.at[k - 1], d)
        c.start()
        sent.append(c)
    for k in (4, 3, 5, 2, 6, 1, 7):
        src = lax.rem(me.y + NY - k, NY)
        rows = pl.ds(pl.multiple_of(base + src * 32, 32), 32)
        remote(gbuf.at[rows], gbuf.at[rows], gs_sem.at[k - 1], gr_sem.at[k - 1], cpeer).wait_recv()
    own = pl.ds(pl.multiple_of(base, 256), 256)
    other = pl.ds(pl.multiple_of(me.core * 512 + (1 - me.xh) * 256, 256), 256)
    c = remote(gbuf.at[own], gbuf.at[own], hs_sem, hr_sem, hpeer)
    c.start()
    sent.append(c)
    c = remote(gbuf.at[own], gbuf.at[own], ks_sem.at[0], kr_sem.at[0], cpeer)
    c.start()
    sent.append(c)
    remote(gbuf.at[other], gbuf.at[other], hs_sem, hr_sem, hpeer).wait_recv()
    c = remote(gbuf.at[other], gbuf.at[other], ks_sem.at[1], kr_sem.at[1], cpeer)
    c.start()
    sent.append(c)
    for q, xh in ((0, me.xh), (1, 1 - me.xh)):
        rows = pl.ds(pl.multiple_of(oc * 512 + xh * 256, 256), 256)
        remote(gbuf.at[rows], gbuf.at[rows], ks_sem.at[q], kr_sem.at[q], cpeer).wait_recv()
    for c in sent:
        c.wait_send()
    load.wait()
    grad = gbuf[...]
    grafted = grad / jnp.sqrt(acc_ref[...] + grad * grad)
    gnorm = jnp.sum(grafted * grafted)
    highest = lax.Precision.HIGHEST
    right = right_ref[...]

    def body(i, tot):
        rows = pl.ds(pl.multiple_of(i * 256, 256), 256)
        v = jnp.dot(left_ref[rows], gbuf[...], precision=highest, preferred_element_type=F32)
        v = jnp.dot(v, right, precision=highest, preferred_element_type=F32)
        cond[rows] = v
        return tot + jnp.sum(v * v)

    cnorm = lax.fori_loop(0, 4, body, jnp.float32(0.0))
    factor = jnp.sqrt(gnorm) / jnp.sqrt(cnorm + 1e-06)
    out_ref[...] = cond[...] * factor


def reduce_and_step(terms, left, right, accum):
    dma = pltpu.SemaphoreType.DMA
    vm = pl.BlockSpec(memory_space=pltpu.VMEM)
    return pl.pallas_call(
        reduce_kernel,
        out_shape=jax.ShapeDtypeStruct((1024, 128), F32),
        in_specs=[vm, pl.BlockSpec(memory_space=pl.ANY), vm, vm],
        out_specs=vm,
        scratch_shapes=[
            pltpu.VMEM((1024, 1024), F32),
            pltpu.VMEM((2, 512, 128), F32),
            pltpu.VMEM((2, 512, 128), F32),
            pltpu.VMEM((3, 256, 128), BF16),
            pltpu.VMEM((3, 256, 128), BF16),
            pltpu.VMEM((256, 128), F32),
            pltpu.VMEM((256, 128), BF16),
            pltpu.VMEM((NY - 1, 32, 128), BF16),
            pltpu.VMEM((NZ, 32, 128), BF16),
            pltpu.VMEM((1024, 128), F32),
            pltpu.VMEM((1024, 128), F32),
            dma, dma((2,)), dma((2,)), dma((3,)), dma((3,)),
            dma((NY - 1,)), dma((NY - 1,)), dma((NZ - 1,)), dma((NZ - 1,)),
            dma((NY - 1,)), dma((NY - 1,)), dma, dma, dma((2,)), dma((2,)),
        ],
        compiler_params=pltpu.CompilerParams(
            collective_id=0, has_side_effects=True, vmem_limit_bytes=48 << 20
        ),
    )(terms, left, right, accum)


def on_device(
    img_resid, img_hidden, txt_resid, txt_hidden, edge_weight, left_root, right_root, graft_acc
):
    split_at = img_hidden.shape[1]
    opt_pos = lax.axis_index("opt")
    img_count = img_resid.shape[0]
    txt_count = txt_resid.shape[0]
    img_dir, img_len = embed_rows(img_resid, img_hidden, edge_weight[0], split_at)
    img_emb = img_dir.astype(BF16)
    visitors = [img_emb] + [shifted(img_emb, "dp", -c) for c in range(1, WINDOW)]
    txt_dir, txt_len = embed_rows(txt_resid, txt_hidden, edge_weight[1], split_at)
    txt_emb = txt_dir.astype(BF16)
    row_start = opt_pos * img_count
    eye = (
        row_start + lax.broadcasted_iota(jnp.int32, (img_count, txt_count), 0)
        == lax.broadcasted_iota(jnp.int32, (img_count, txt_count), 1)
    ).astype(F32)
    txt_part = jnp.zeros((txt_count, split_at // 8), F32)
    txt_rad = jnp.zeros((txt_count,), F32)
    img_part = jnp.zeros((img_count + 8, split_at // 8), F32)
    for c in range(WINDOW):
        sims = jnp.dot(visitors[c], txt_emb.T, preferred_element_type=F32)
        probs = jax.nn.sigmoid(10.0 * sims - 2.0)
        if c == 0:
            probs = probs - eye
        wts = probs.astype(BF16)
        ws = wts.astype(F32) * sims
        back = jnp.concatenate(
            [
                jnp.dot(wts, txt_emb[:, split_at:], preferred_element_type=F32),
                jnp.broadcast_to(jnp.sum(ws, axis=1)[None], (8, img_count)),
            ]
        )
        img_part = img_part + (shifted(back, "dp", c) if c else back)
        txt_part = txt_part + jnp.dot(
            wts.T, visitors[c][:, split_at:], preferred_element_type=F32
        )
        txt_rad = txt_rad + jnp.sum(ws, axis=0)
    img_dz = edge_back(
        img_dir, img_len, img_part[:img_count], img_part[img_count][:, None], split_at
    )
    other = (1 - opt_pos) * img_count
    away = jnp.concatenate(
        [
            lax.dynamic_slice_in_dim(txt_part, other, img_count, 0),
            jnp.broadcast_to(lax.dynamic_slice_in_dim(txt_rad, other, img_count, 0)[None], (8, img_count)),
        ]
    )
    came = lax.ppermute(away, "opt", [(0, 1), (1, 0)])
    txt_rows = lax.dynamic_slice_in_dim(txt_hidden, row_start, img_count, 0)
    own_grad = lax.dynamic_slice_in_dim(txt_part, row_start, img_count, 0) + came[:img_count]
    own_rad = lax.dynamic_slice_in_dim(txt_rad, row_start, img_count, 0) + came[img_count]
    own_dir = lax.dynamic_slice_in_dim(txt_dir, row_start, img_count, 0)
    own_len = lax.dynamic_slice_in_dim(txt_len, row_start, img_count, 0)
    txt_dz = edge_back(own_dir, own_len, own_grad, own_rad[:, None], split_at)
    terms = jnp.stack(
        [
            jnp.dot(img_hidden.T, img_dz, preferred_element_type=F32),
            jnp.dot(txt_rows.T, txt_dz, preferred_element_type=F32),
        ]
    )
    return reduce_and_step(terms, left_root[0], right_root[0], graft_acc[0])[None]


def solution(mesh):
    placed = (
        P(("dp", "opt"), None),
        P(("dp", "opt"), None),
        P("dp", None),
        P("dp", None),
        P(),
        P("opt", None, None),
        P("opt", None, None),
        P("opt", None, None),
    )
    return jax.shard_map(
        on_device, mesh=mesh, in_specs=placed, out_specs=P("opt", None, None), check_vma=False
    )
```

```python
import jax
import jax.numpy as jnp
from jax import lax
from jax.experimental import pallas as pl
from jax.experimental.pallas import tpu as pltpu
from jax.sharding import PartitionSpec as P

NX, NY, NZ, NDP = 2, 8, 12, 384
D, BLK, EDGE = 1152, 1024, 128
ROWS, TXT = 128, 256
MESH = pl.DeviceIdType.MESH
F32 = jnp.float32
BF16 = jnp.bfloat16
YORDER = (4, 3, 5, 2, 6, 1, 7)
ZORDER = (6, 5, 7, 4, 8, 3, 9, 2, 10, 1, 11)


def rows_at(start, size):
    return pl.ds(pl.multiple_of(start, size), size)


def dot(a, b, dims=(1, 0)):
    return lax.dot_general(
        a, b, (((dims[0],), (dims[1],)), ((), ())), preferred_element_type=F32
    )


def kernel(
    img_resid, img_hidden, txt_resid, txt_hidden, edge_weight, left_hbm, right_hbm, acc_hbm,
    out_ref,
    ir, ih, tr, th, ew, left, right, acc,
    emb, idir, ilen, temb, tdir, tlen, vis, back, back_in, tout, tin, iht, tht, lhi, llo,
    p, cbuf, acc1, xsend, xbuf, acc2, ysend, ybuf, zbuf, gbuf, cond,
    load_sem, vs_sem, vr_sem, bs_sem, br_sem, ts_sem, tr_sem,
    cs_sem, cr_sem, xs_sem, xr_sem, ys_sem, yr_sem, zs_sem, zr_sem,
    gs_sem, gr_sem, hs_sem, hr_sem, ks_sem, kr_sem,
):
    dp = lax.axis_index("dp")
    xl = lax.axis_index("opt")
    core = lax.rem(dp, 2)
    y = lax.rem(lax.div(dp, 2), NY)
    z = lax.rem(lax.div(dp, 2 * NY), NZ)
    xh = lax.div(dp, 2 * NY * NZ)
    oc = 1 - core

    def at(xh=xh, z=z, y=y, core=core, xl=xl):
        return (((xh * NZ + z) * NY + y) * 2 + core, xl)

    loads = []
    for n, (src, dst) in enumerate([
        (img_hidden, ih), (edge_weight.at[0], ew.at[0]), (img_resid, ir),
        (txt_hidden, th), (edge_weight.at[1], ew.at[1]), (txt_resid, tr),
        (left_hbm, left), (right_hbm, right), (acc_hbm, acc),
    ]):
        c = pltpu.make_async_copy(src, dst, load_sem.at[n])
        c.start()
        loads.append(c)

    x = xh * 2 + xl
    xpeer = []
    for k in range(1, 4):
        px = lax.rem(x + k, 4)
        xpeer.append((px, at(xh=lax.div(px, 2), xl=lax.rem(px, 2))))
    ypeer = [(lax.rem(y + k, NY), at(y=lax.rem(y + k, NY))) for k in range(1, NY)]
    zpeer = [(lax.rem(z + k, NZ), at(z=lax.rem(z + k, NZ))) for k in range(1, NZ)]
    cpeer = at(core=oc)
    hpeer = at(xh=1 - xh)
    opeer = (dp, 1 - xl)
    before = [(lax.rem(dp + NDP - c, NDP), xl) for c in (1, 2)]
    after = [(lax.rem(dp + c, NDP), xl) for c in (1, 2)]
    side = (lax.rem(dp + NDP + 2 * core - 1, NDP), xl)

    barrier = pltpu.get_barrier_semaphore()
    peers = [before[1], after[1], side, cpeer] + [d for _, d in xpeer + ypeer + zpeer]
    for d in peers:
        pl.semaphore_signal(barrier, inc=1, device_id=d, device_id_type=MESH)

    def remote(src, dst, s, r, d):
        return pltpu.make_async_remote_copy(
            src_ref=src, dst_ref=dst, send_sem=s, recv_sem=r, device_id=d, device_id_type=MESH
        )

    sent = []

    def send(*args):
        c = remote(*args)
        c.start()
        sent.append(c)
        return c

    def embed(resid, hidden, weight, emb_out, dir_out, len_out):
        edge = dot(hidden[...], weight[...]) + resid[:, BLK:].astype(F32)
        body = resid[:, :BLK].astype(F32)
        square = jnp.sum(body * body, axis=1, keepdims=True) + jnp.sum(
            edge * edge, axis=1, keepdims=True
        )
        length = jnp.sqrt(square + 1e-06)
        inverse = 1.0 / length
        emb_out[:, :BLK] = (body * inverse).astype(BF16)
        direction = edge * inverse
        emb_out[:, BLK:] = direction.astype(BF16)
        dir_out[...] = direction
        len_out[...] = jnp.broadcast_to(inverse, len_out.shape)

    for n in range(3):
        loads[n].wait()
    embed(ir, ih, ew.at[0], emb, idir, ilen)
    pl.semaphore_wait(barrier, len(peers))

    send(emb, vis.at[1], vs_sem.at[1], vr_sem.at[1], before[1])
    pair_copy = remote(emb, vis.at[0], vs_sem.at[0], vr_sem.at[0], cpeer)

    @pl.when(core == 1)
    def _():
        pair_copy.start()

    for n in range(3, 6):
        loads[n].wait()
    embed(tr, th, ew.at[1], temb, tdir, tlen)

    def pair(view, diagonal):
        images = view[...]
        sims = dot(temb[...], images, (1, 1))
        probs = 1.0 / (1.0 + jnp.exp(2.0 - 10.0 * sims))
        if diagonal:
            text = lax.broadcasted_iota(jnp.int32, sims.shape, 0)
            image = lax.broadcasted_iota(jnp.int32, sims.shape, 1) + xl * ROWS
            probs = probs - (text == image).astype(F32)
        weights = probs.astype(BF16)
        radial = weights.astype(F32) * sims
        txt_edge = dot(weights, images[:, BLK:])
        txt_radial = jnp.sum(radial, axis=1, keepdims=True)
        img_edge = dot(weights, temb[:, BLK:], (0, 0))
        img_radial = jnp.sum(radial, axis=0, keepdims=True)
        return img_edge, img_radial, txt_edge - tdir[...] * txt_radial

    own_edge, own_radial, txt_total = pair(emb, True)
    back[2, :ROWS] = own_edge
    back[2, ROWS:] = jnp.broadcast_to(own_radial, (8, EDGE))
    tout[...] = txt_total
    iht[...] = ih[...].T
    tht[...] = th[rows_at(xl * ROWS, ROWS)].T

    for turn in range(2):
        slot = core if turn == 0 else oc
        far = remote(vis.at[slot], vis.at[slot], vs_sem.at[slot], vr_sem.at[slot], cpeer)
        far.wait_recv()
        if turn == 1:
            onward = remote(vis.at[1], vis.at[0], vs_sem.at[0], vr_sem.at[0], cpeer)

            @pl.when(core == 0)
            def _():
                onward.start()

        edge, radial, txt_edge = pair(vis.at[slot], False)
        back[slot, :ROWS] = edge
        back[slot, ROWS:] = jnp.broadcast_to(radial, (8, EDGE))
        send(
            back.at[slot], back_in.at[slot], bs_sem.at[slot], br_sem.at[slot],
            (lax.rem(dp + slot + 1, NDP), xl),
        )
        tout[...] = tout[...] + txt_edge
    sent.append(pair_copy)
    send(tout.at[rows_at((1 - xl) * ROWS, ROWS)], tin, ts_sem, tr_sem, opeer)

    loads[6].wait()

    @pl.loop(0, 8)
    def _(i):
        r = rows_at(i * 128, 128)
        value = left[r]
        high = value.astype(BF16)
        lhi[r] = high
        llo[r] = (value - high.astype(F32)).astype(BF16)

    mine = rows_at(core * 512, 512)
    theirs = rows_at(oc * 512, 512)
    for slot in range(2):
        remote(
            back.at[slot], back_in.at[slot], bs_sem.at[slot], br_sem.at[slot], cpeer
        ).wait_recv()
    total = back[2] + back_in[0] + back_in[1]
    radial = jnp.broadcast_to(total[ROWS:ROWS + 1], (ROWS, EDGE)).T
    dz = ((total[:ROWS] - idir[...] * radial) * ilen[...]).astype(BF16)
    p[0, theirs] = dot(iht[theirs], dz)
    ccopies = [send(p.at[0, theirs], cbuf.at[0], cs_sem.at[0], cr_sem.at[0], cpeer)]
    p[0, mine] = dot(iht[mine], dz)
    remote(tin, tin, ts_sem, tr_sem, opeer).wait_recv()
    own = rows_at(xl * ROWS, ROWS)
    dz = ((tout[own] + tin[...]) * tlen[own]).astype(BF16)
    p[1, theirs] = dot(tht[theirs], dz)
    ccopies.append(send(p.at[1, theirs], cbuf.at[1], cs_sem.at[1], cr_sem.at[1], cpeer))
    p[1, mine] = dot(tht[mine], dz)

    for t in range(2):
        ccopies[t].wait_recv()
        acc1[t] = p[t, mine] + cbuf[t]
    xcopies = []
    for k in (2, 1, 3):
        px, d = xpeer[k - 1]
        xsend[k - 1] = acc1[lax.rem(px, 2), rows_at(lax.div(px, 2) * 256, 256)].astype(BF16)
        xcopies.append(send(xsend.at[k - 1], xbuf.at[k - 1], xs_sem.at[k - 1], xr_sem.at[k - 1], d))
    total = acc1[xl, rows_at(xh * 256, 256)]
    for c in xcopies:
        c.wait_recv()
    for k in range(3):
        total = total + xbuf[k].astype(F32)
    acc2[...] = total
    ysend[...] = total.astype(BF16)
    ycopies = []
    for k in YORDER:
        py, d = ypeer[k - 1]
        ycopies.append(send(
            ysend.at[rows_at(py * 32, 32)], ybuf.at[k - 1], ys_sem.at[k - 1], yr_sem.at[k - 1], d
        ))
    part = acc2[rows_at(y * 32, 32)]
    for c in ycopies:
        c.wait_recv()
    for k in range(NY - 1):
        part = part + ybuf[k].astype(F32)
    zbuf[z] = part.astype(BF16)
    for k in ZORDER:
        send(zbuf.at[z], zbuf.at[z], zs_sem.at[k - 1], zr_sem.at[k - 1], zpeer[k - 1][1])
    for k in ZORDER:
        src = lax.rem(z + NZ - k, NZ)
        remote(zbuf.at[src], zbuf.at[src], zs_sem.at[k - 1], zr_sem.at[k - 1], cpeer).wait_recv()
    part = zbuf[0].astype(F32)
    for k in range(1, NZ):
        part = part + zbuf[k].astype(F32)
    base = core * 512 + xh * 256
    own = rows_at(base + y * 32, 32)
    gbuf[own] = part
    for k in YORDER:
        send(gbuf.at[own], gbuf.at[own], gs_sem.at[k - 1], gr_sem.at[k - 1], ypeer[k - 1][1])
    for k in YORDER:
        src = lax.rem(y + NY - k, NY)
        r = rows_at(base + src * 32, 32)
        remote(gbuf.at[r], gbuf.at[r], gs_sem.at[k - 1], gr_sem.at[k - 1], cpeer).wait_recv()
    own = rows_at(base, 256)
    other = rows_at(core * 512 + (1 - xh) * 256, 256)
    send(gbuf.at[own], gbuf.at[own], hs_sem, hr_sem, hpeer)
    send(gbuf.at[own], gbuf.at[own], ks_sem.at[0], kr_sem.at[0], cpeer)

    def quarter(r, first):
        g = gbuf[r]
        high = g.astype(BF16)
        low = (g - high.astype(F32)).astype(BF16)
        both = jnp.concatenate([high, low], axis=1)

        @pl.loop(0, 4)
        def _(i):
            o = rows_at(i * 256, 256)
            lh = lhi[o, r]
            v = dot(lh, both)
            v = v[:, :EDGE] + v[:, EDGE:] + dot(llo[o, r], high)
            cond[o] = v if first else cond[o] + v

    quarter(own, True)
    remote(gbuf.at[other], gbuf.at[other], hs_sem, hr_sem, hpeer).wait_recv()
    send(gbuf.at[other], gbuf.at[other], ks_sem.at[1], kr_sem.at[1], cpeer)
    quarter(other, False)
    for q, h in ((0, xh), (1, 1 - xh)):
        r = rows_at(oc * 512 + h * 256, 256)
        remote(gbuf.at[r], gbuf.at[r], ks_sem.at[q], kr_sem.at[q], cpeer).wait_recv()
        quarter(r, False)
    loads[7].wait()
    loads[8].wait()
    r = right[...]
    rhi = r.astype(BF16)
    rlo = (r - rhi.astype(F32)).astype(BF16)
    rboth = jnp.concatenate([rhi, rlo], axis=1)

    def body(i, sums):
        o = rows_at(i * 256, 256)
        v = cond[o]
        high = v.astype(BF16)
        low = (v - high.astype(F32)).astype(BF16)
        w = dot(high, rboth)
        w = w[:, :EDGE] + w[:, EDGE:] + dot(low, rhi)
        cond[o] = w
        g = gbuf[o]
        return sums[0] + jnp.sum(g * g / (acc[o] + g * g)), sums[1] + jnp.sum(w * w)

    gsum, csum = lax.fori_loop(0, 4, body, (jnp.float32(0.0), jnp.float32(0.0)))
    factor = jnp.sqrt(gsum) / jnp.sqrt(csum + 1e-06)
    out_ref[...] = cond[...] * factor
    for c in sent:
        c.wait_send()


def on_device(*args):
    dma = pltpu.SemaphoreType.DMA
    hbm = pl.BlockSpec(memory_space=pl.ANY)

    def f32(*shape):
        return pltpu.VMEM(shape, F32)

    def bf16(*shape):
        return pltpu.VMEM(shape, BF16)

    args = args[:5] + tuple(a.reshape(a.shape[1:]) for a in args[5:])
    out = pl.pallas_call(
        kernel,
        out_shape=jax.ShapeDtypeStruct((BLK, EDGE), F32),
        in_specs=[hbm] * 8,
        out_specs=pl.BlockSpec(memory_space=pltpu.VMEM),
        scratch_shapes=[
            bf16(ROWS, D), bf16(ROWS, BLK), bf16(TXT, D), bf16(TXT, BLK), bf16(2, BLK, EDGE),
            f32(BLK, BLK), f32(EDGE, EDGE), f32(BLK, EDGE),
            bf16(ROWS, D), f32(ROWS, EDGE), f32(ROWS, EDGE),
            bf16(TXT, D), f32(TXT, EDGE), f32(TXT, EDGE),
            bf16(2, ROWS, D), f32(3, ROWS + 8, EDGE), f32(2, ROWS + 8, EDGE),
            f32(TXT, EDGE), f32(ROWS, EDGE), bf16(BLK, ROWS), bf16(BLK, ROWS),
            bf16(BLK, BLK), bf16(BLK, BLK),
            f32(2, BLK, EDGE), f32(2, 512, EDGE), f32(2, 512, EDGE),
            bf16(3, 256, EDGE), bf16(3, 256, EDGE), f32(256, EDGE),
            bf16(256, EDGE), bf16(NY - 1, 32, EDGE), bf16(NZ, 32, EDGE),
            f32(BLK, EDGE), f32(BLK, EDGE),
            dma((9,)), dma((2,)), dma((2,)), dma((2,)), dma((2,)), dma, dma,
            dma((2,)), dma((2,)), dma((3,)), dma((3,)), dma((NY - 1,)), dma((NY - 1,)),
            dma((NZ - 1,)), dma((NZ - 1,)), dma((NY - 1,)), dma((NY - 1,)),
            dma, dma, dma((2,)), dma((2,)),
        ],
        compiler_params=pltpu.CompilerParams(
            collective_id=0, has_side_effects=True, vmem_limit_bytes=48 << 20
        ),
    )(*args)
    return out[None]


def solution(mesh):
    placed = (
        P(("dp", "opt"), None),
        P(("dp", "opt"), None),
        P("dp", None),
        P("dp", None),
        P(),
        P("opt", None, None),
        P("opt", None, None),
        P("opt", None, None),
    )
    return jax.shard_map(
        on_device, mesh=mesh, in_specs=placed, out_specs=P("opt", None, None), check_vma=False
    )
```

```python
import jax
import jax.numpy as jnp
from jax import lax
from jax.experimental import pallas as pl
from jax.experimental.pallas import tpu as pltpu
from jax.sharding import PartitionSpec as P

NX, NY, NZ, NDP = 2, 8, 12, 384
D, BLK, EDGE = 1152, 1024, 128
ROWS, TXT = 128, 256
MESH = pl.DeviceIdType.MESH
F32 = jnp.float32
BF16 = jnp.bfloat16
YORDER = (4, 3, 5, 2, 6, 1, 7)
ZORDER = (6, 5, 7, 4, 8, 3, 9, 2, 10, 1, 11)


def rows_at(start, size):
    return pl.ds(pl.multiple_of(start, size), size)


def dot(a, b, dims=(1, 0)):
    return lax.dot_general(
        a, b, (((dims[0],), (dims[1],)), ((), ())), preferred_element_type=F32
    )


def kernel(
    img_resid, img_hidden, txt_resid, txt_hidden, edge_weight, left_hbm, right_hbm, acc_hbm,
    out_ref, factor_ref,
    ir, ih, tr, th, ew, left, right, acc,
    emb, idir, ilen, temb, tdir, tlen, vis, back, back_in, tout, tin, iht, tht, lhi, llo,
    p, cbuf, acc1, xsend, xbuf, acc2, ysend, ybuf, zsend, zbuf, gbuf, cond,
    load_sem, vs_sem, vr_sem, bs_sem, br_sem, ts_sem, tr_sem,
    cs_sem, cr_sem, xs_sem, xr_sem, ys_sem, yr_sem, zs_sem, zr_sem,
    gs_sem, gr_sem, hs_sem, hr_sem, ks_sem, kr_sem,
):
    dp = lax.axis_index("dp")
    xl = lax.axis_index("opt")
    core = lax.rem(dp, 2)
    y = lax.rem(lax.div(dp, 2), NY)
    z = lax.rem(lax.div(dp, 2 * NY), NZ)
    xh = lax.div(dp, 2 * NY * NZ)
    oc = 1 - core

    def at(xh=xh, z=z, y=y, core=core, xl=xl):
        return (((xh * NZ + z) * NY + y) * 2 + core, xl)

    loads = []
    for n, (src, dst) in enumerate([
        (img_hidden, ih), (edge_weight.at[0], ew.at[0]), (img_resid, ir),
        (txt_hidden, th), (edge_weight.at[1], ew.at[1]), (txt_resid, tr),
        (left_hbm, left), (right_hbm, right), (acc_hbm, acc),
    ]):
        c = pltpu.make_async_copy(src, dst, load_sem.at[n])
        c.start()
        loads.append(c)

    x = xh * 2 + xl
    xpeer = []
    for k in range(1, 4):
        px = lax.rem(x + k, 4)
        xpeer.append((px, at(xh=lax.div(px, 2), xl=lax.rem(px, 2))))
    ypeer = [(lax.rem(y + k, NY), at(y=lax.rem(y + k, NY))) for k in range(1, NY)]
    zpeer = [(lax.rem(z + k, NZ), at(z=lax.rem(z + k, NZ))) for k in range(1, NZ)]
    cpeer = at(core=oc)
    hpeer = at(xh=1 - xh)
    opeer = (dp, 1 - xl)

    def along(c):
        there = lax.rem(dp + NDP + c, NDP)
        return there, lax.rem(xl + xh + lax.div(there, 2 * NY * NZ), 2)

    after = [along(1), along(2)]
    side = along(2 * core - 1)
    zn = z + 1 - 2 * lax.rem(z, 2)
    npeer = [hpeer, at(z=zn), at(xh=1 - xh, z=zn)]

    barrier = pltpu.get_barrier_semaphore()
    peers = [along(-2), after[1], side, cpeer, npeer[2]] + [d for _, d in xpeer + ypeer + zpeer]
    for d in peers:
        pl.semaphore_signal(barrier, inc=1, device_id=d, device_id_type=MESH)

    def remote(src, dst, s, r, d):
        return pltpu.make_async_remote_copy(
            src_ref=src, dst_ref=dst, send_sem=s, recv_sem=r, device_id=d, device_id_type=MESH
        )

    sent = []

    def send(*args):
        c = remote(*args)
        c.start()
        sent.append(c)
        return c

    def embed(resid, hidden, weight, emb_out, dir_out, len_out):
        edge = dot(hidden[...], weight[...]) + resid[:, BLK:].astype(F32)
        body = resid[:, :BLK].astype(F32)
        square = jnp.sum(body * body, axis=1, keepdims=True) + jnp.sum(
            edge * edge, axis=1, keepdims=True
        )
        length = jnp.sqrt(square + 1e-06)
        inverse = 1.0 / length
        emb_out[:, :BLK] = (body * inverse).astype(BF16)
        direction = edge * inverse
        emb_out[:, BLK:] = direction.astype(BF16)
        dir_out[...] = direction
        len_out[...] = jnp.broadcast_to(inverse, len_out.shape)

    for n in range(3):
        loads[n].wait()
    embed(ir, ih, ew.at[0], emb, idir, ilen)
    pl.semaphore_wait(barrier, len(peers))

    far_copy = remote(emb, vis.at[1], vs_sem.at[1], vr_sem.at[1], along(-2))
    near_copy = remote(emb, vis.at[0], vs_sem.at[0], vr_sem.at[0], cpeer)
    onward = remote(vis.at[1], vis.at[0], vs_sem.at[0], vr_sem.at[0], cpeer)

    @pl.when(core == 0)
    def _():
        far_copy.start()

    @pl.when(core == 1)
    def _():
        near_copy.start()

    for n in range(3, 6):
        loads[n].wait()
    embed(tr, th, ew.at[1], temb, tdir, tlen)

    @pl.when(core == 1)
    def _():
        far_copy.start()

    def pair(view, diagonal):
        images = view[...]
        sims = dot(temb[...], images, (1, 1))
        probs = 1.0 / (1.0 + jnp.exp(2.0 - 10.0 * sims))
        if diagonal:
            text = lax.broadcasted_iota(jnp.int32, sims.shape, 0)
            image = lax.broadcasted_iota(jnp.int32, sims.shape, 1) + xl * ROWS
            probs = probs - (text == image).astype(F32)
        weights = probs.astype(BF16)
        radial = weights.astype(F32) * sims
        txt_edge = dot(weights, images[:, BLK:])
        txt_radial = jnp.sum(radial, axis=1, keepdims=True)
        img_edge = dot(weights, temb[:, BLK:], (0, 0))
        img_radial = jnp.sum(radial, axis=0, keepdims=True)
        return img_edge, img_radial, txt_edge - tdir[...] * txt_radial

    own_edge, own_radial, txt_total = pair(emb, True)
    back[2, :ROWS] = own_edge
    back[2, ROWS:] = jnp.broadcast_to(own_radial, (8, EDGE))
    tout[...] = txt_total

    @pl.when(core == 0)
    def _():
        far_copy.wait_recv()
        onward.start()

    for slot in range(2):
        if slot == 0:
            near_copy.wait_recv()
        else:
            @pl.when(core == 1)
            def _():
                far_copy.wait_recv()

        edge, radial, txt_edge = pair(vis.at[slot], False)
        back[slot, :ROWS] = edge
        back[slot, ROWS:] = jnp.broadcast_to(radial, (8, EDGE))
        send(back.at[slot], back_in.at[slot], bs_sem.at[slot], br_sem.at[slot], after[slot])
        tout[...] = tout[...] + txt_edge
    sent.append(far_copy)
    sent.append(near_copy)
    send(tout.at[rows_at((1 - xl) * ROWS, ROWS)], tin, ts_sem, tr_sem, opeer)
    iht[...] = ih[...].T
    tht[...] = th[rows_at(xl * ROWS, ROWS)].T

    mine = rows_at(core * 512, 512)
    theirs = rows_at(oc * 512, 512)
    for slot in range(2):
        remote(
            back.at[slot], back_in.at[slot], bs_sem.at[slot], br_sem.at[slot], cpeer
        ).wait_recv()
    total = back[2] + back_in[0] + back_in[1]
    radial = jnp.broadcast_to(total[ROWS:ROWS + 1], (ROWS, EDGE)).T
    dz = ((total[:ROWS] - idir[...] * radial) * ilen[...]).astype(BF16)
    p[0, theirs] = dot(iht[theirs], dz)
    ccopies = [send(p.at[0, theirs], cbuf.at[0], cs_sem.at[0], cr_sem.at[0], cpeer)]
    p[0, mine] = dot(iht[mine], dz)
    remote(tin, tin, ts_sem, tr_sem, opeer).wait_recv()
    own = rows_at(xl * ROWS, ROWS)
    dz = ((tout[own] + tin[...]) * tlen[own]).astype(BF16)
    p[1, theirs] = dot(tht[theirs], dz)
    ccopies.append(send(p.at[1, theirs], cbuf.at[1], cs_sem.at[1], cr_sem.at[1], cpeer))
    p[1, mine] = dot(tht[mine], dz)

    for t in range(2):
        ccopies[t].wait_recv()
        acc1[t] = (p[t, mine] + cbuf[t]).reshape(NY, 2, 32, EDGE)
        for h in (1, 0):
            k = lax.rem(2 * h + t + 4 - x, 4)
            slot = lax.max(k - 1, 0)

            @pl.when(k > 0)
            def _():
                xsend[slot] = acc1[t, :, h].astype(BF16)
                remote(
                    xsend.at[slot], xbuf.at[slot], xs_sem.at[slot], xr_sem.at[slot],
                    at(xh=h, xl=t),
                ).start()

    loads[6].wait()

    @pl.loop(0, 8)
    def _(i):
        r = rows_at(i * 128, 128)
        value = left[r]
        high = value.astype(BF16)
        lhi[r] = high
        llo[r] = (value - high.astype(F32)).astype(BF16)

    total = acc1[xl, :, xh]
    for k in range(3):
        c = remote(xsend.at[k], xbuf.at[k], xs_sem.at[k], xr_sem.at[k], cpeer)
        c.wait_recv()
        sent.append(c)
        total = total + xbuf[k].astype(F32)
    acc2[...] = total
    ysend[...] = total.astype(BF16)
    ycopies = []
    for k in YORDER:
        py, d = ypeer[k - 1]
        ycopies.append(send(
            ysend.at[py], ybuf.at[k - 1], ys_sem.at[k - 1], yr_sem.at[k - 1], d
        ))
    part = acc2[y]
    for c in ycopies:
        c.wait_recv()
    for k in range(NY - 1):
        part = part + ybuf[k].astype(F32)
    zsend[...] = part.astype(BF16).reshape(2, 16, EDGE)
    for k in ZORDER:
        pz, d = zpeer[k - 1]
        send(zsend.at[lax.rem(pz, 2)], zbuf.at[z], zs_sem.at[k - 1], zr_sem.at[k - 1], d)
    zh = lax.rem(z, 2)
    zbuf[z] = zsend[zh]
    for k in ZORDER:
        src = lax.rem(z + NZ - k, NZ)
        remote(zbuf.at[src], zbuf.at[src], zs_sem.at[k - 1], zr_sem.at[k - 1], cpeer).wait_recv()
    part = zbuf[0].astype(F32)
    for k in range(1, NZ):
        part = part + zbuf[k].astype(F32)
    at_y = core * NY + y
    gbuf[at_y, xh, zh] = part.astype(BF16)
    own = gbuf.at[at_y, xh, zh]
    for k, d in enumerate(npeer):
        send(own, own, hs_sem.at[k], hr_sem.at[k], d)
    for k, (h, q) in enumerate(((1 - xh, zh), (xh, 1 - zh), (1 - xh, 1 - zh))):
        came = gbuf.at[at_y, h, q]
        remote(came, came, hs_sem.at[k], hr_sem.at[k], cpeer).wait_recv()
    own = gbuf.at[at_y]
    for k in YORDER:
        send(own, own, gs_sem.at[k - 1], gr_sem.at[k - 1], ypeer[k - 1][1])
    for k in YORDER:
        came = gbuf.at[core * NY + lax.rem(y + NY - k, NY)]
        remote(came, came, gs_sem.at[k - 1], gr_sem.at[k - 1], cpeer).wait_recv()
    own = gbuf.at[pl.ds(core * NY, NY)]
    send(own, own, ks_sem, kr_sem, cpeer)

    def half(c, first):
        g = gbuf[pl.ds(c * NY, NY)].reshape(512, EDGE)
        r = rows_at(c * 512, 512)

        @pl.loop(0, 4)
        def _(i):
            o = rows_at(i * 256, 256)
            v = dot(lhi[o, r], g) + dot(llo[o, r], g)
            cond[o] = v if first else cond[o] + v

    half(core, True)
    loads[7].wait()
    loads[8].wait()
    other = gbuf.at[pl.ds(oc * NY, NY)]
    remote(other, other, ks_sem, kr_sem, cpeer).wait_recv()
    half(oc, False)
    r = right[...]
    rhi = r.astype(BF16)
    rlo = (r - rhi.astype(F32)).astype(BF16)
    rboth = jnp.concatenate([rhi, rlo], axis=1)

    def body(i, sums):
        o = rows_at(i * 256, 256)
        v = cond[o]
        high = v.astype(BF16)
        low = (v - high.astype(F32)).astype(BF16)
        w = dot(high, rboth)
        w = w[:, :EDGE] + w[:, EDGE:] + dot(low, rhi)
        out_ref[o] = w
        g = gbuf[pl.ds(i * 4, 4)].reshape(256, EDGE).astype(F32)
        return sums[0] + jnp.sum(g * g / (acc[o] + g * g)), sums[1] + jnp.sum(w * w)

    gsum, csum = lax.fori_loop(0, 4, body, (jnp.float32(0.0), jnp.float32(0.0)))
    factor = jnp.sqrt(gsum) / jnp.sqrt(csum + 1e-06)
    factor_ref[...] = jnp.broadcast_to(factor, factor_ref.shape)
    for c in sent:
        c.wait_send()


def on_device(*args):
    dma = pltpu.SemaphoreType.DMA
    hbm = pl.BlockSpec(memory_space=pl.ANY)

    def f32(*shape):
        return pltpu.VMEM(shape, F32)

    def bf16(*shape):
        return pltpu.VMEM(shape, BF16)

    args = args[:5] + tuple(a.reshape(a.shape[1:]) for a in args[5:])
    out, factor = pl.pallas_call(
        kernel,
        out_shape=[
            jax.ShapeDtypeStruct((BLK, EDGE), F32), jax.ShapeDtypeStruct((8, EDGE), F32)
        ],
        in_specs=[hbm] * 8,
        out_specs=[pl.BlockSpec(memory_space=pltpu.VMEM)] * 2,
        scratch_shapes=[
            bf16(ROWS, D), bf16(ROWS, BLK), bf16(TXT, D), bf16(TXT, BLK), bf16(2, BLK, EDGE),
            f32(BLK, BLK), f32(EDGE, EDGE), f32(BLK, EDGE),
            bf16(ROWS, D), f32(ROWS, EDGE), f32(ROWS, EDGE),
            bf16(TXT, D), f32(TXT, EDGE), f32(TXT, EDGE),
            bf16(2, ROWS, D), f32(3, ROWS + 8, EDGE), f32(2, ROWS + 8, EDGE),
            f32(TXT, EDGE), f32(ROWS, EDGE), bf16(BLK, ROWS), bf16(BLK, ROWS),
            bf16(BLK, BLK), bf16(BLK, BLK),
            f32(2, BLK, EDGE), f32(2, 512, EDGE), f32(2, NY, 2, 32, EDGE),
            bf16(3, NY, 32, EDGE), bf16(3, NY, 32, EDGE), f32(NY, 32, EDGE),
            bf16(NY, 32, EDGE), bf16(NY - 1, 32, EDGE), bf16(2, 16, EDGE), bf16(NZ, 16, EDGE),
            bf16(2 * NY, 2, 2, 16, EDGE), f32(BLK, EDGE),
            dma((9,)), dma((2,)), dma((2,)), dma((2,)), dma((2,)), dma, dma,
            dma((2,)), dma((2,)), dma((3,)), dma((3,)), dma((NY - 1,)), dma((NY - 1,)),
            dma((NZ - 1,)), dma((NZ - 1,)), dma((NY - 1,)), dma((NY - 1,)),
            dma((3,)), dma((3,)), dma, dma,
        ],
        compiler_params=pltpu.CompilerParams(
            collective_id=0, has_side_effects=True, vmem_limit_bytes=60 << 20
        ),
    )(*args)
    return (out * factor[0, 0])[None]


def solution(mesh):
    placed = (
        P(("dp", "opt"), None),
        P(("dp", "opt"), None),
        P("dp", None),
        P("dp", None),
        P(),
        P("opt", None, None),
        P("opt", None, None),
        P("opt", None, None),
    )
    return jax.shard_map(
        on_device, mesh=mesh, in_specs=placed, out_specs=P("opt", None, None), check_vma=False
    )
```

```python
import jax
import jax.numpy as jnp
from jax import lax
from jax.experimental import pallas as pl
from jax.experimental.pallas import tpu as pltpu
from jax.sharding import PartitionSpec as P

NX, NY, NZ, NDP = 2, 8, 12, 384
D, BLK, EDGE = 1152, 1024, 128
ROWS, TXT = 128, 256
MESH = pl.DeviceIdType.MESH
F32 = jnp.float32
BF16 = jnp.bfloat16
YORDER = (4, 3, 5, 2, 6, 1, 7)
ZORDER = (6, 5, 7, 4, 8, 3, 9, 2, 10, 1, 11)


def rows_at(start, size):
    return pl.ds(pl.multiple_of(start, size), size)


def dot(a, b, dims=(1, 0)):
    return lax.dot_general(
        a, b, (((dims[0],), (dims[1],)), ((), ())), preferred_element_type=F32
    )


def kernel(
    img_resid, img_hidden, txt_resid, txt_hidden, edge_weight, left_hbm, right_hbm, acc_hbm,
    out_ref,
    ir, ih, tr, th, ew, left, right, acc,
    emb, idir, ilen, temb, tdir, tlen, vis, back, back_in, tout, tin, iht, tht, lhi, llo,
    p, cbuf, acc1, xsend, xbuf, acc2, ysend, ybuf, zbuf, gbuf, cond, ready,
    load_sem, vs_sem, vr_sem, bs_sem, br_sem, ts_sem, tr_sem,
    cs_sem, cr_sem, xs_sem, xr_sem, ys_sem, yr_sem, zs_sem, zr_sem,
    gs_sem, gr_sem, ks_sem, kr_sem,
):
    dp = lax.axis_index("dp")
    xl = lax.axis_index("opt")
    core = lax.rem(dp, 2)
    y = lax.rem(lax.div(dp, 2), NY)
    z = lax.rem(lax.div(dp, 2 * NY), NZ)
    xh = lax.div(dp, 2 * NY * NZ)
    oc = 1 - core

    def at(xh=xh, z=z, y=y, core=core, xl=xl):
        return (((xh * NZ + z) * NY + y) * 2 + core, xl)

    loads = []
    for n, (src, dst) in enumerate([
        (img_hidden, ih), (edge_weight.at[0], ew.at[0]), (img_resid, ir),
        (txt_hidden, th), (edge_weight.at[1], ew.at[1]), (txt_resid, tr),
        (left_hbm, left), (right_hbm, right), (acc_hbm, acc),
    ]):
        loads.append(pltpu.make_async_copy(src, dst, load_sem.at[n]))
    for c in loads[:6]:
        c.start()

    x = xh * 2 + xl
    xpeer = []
    for k in range(1, 4):
        px = lax.rem(x + k, 4)
        xpeer.append((px, at(xh=lax.div(px, 2), xl=lax.rem(px, 2))))
    ypeer = [(lax.rem(y + k, NY), at(y=lax.rem(y + k, NY))) for k in range(1, NY)]
    zpeer = [(lax.rem(z + k, NZ), at(z=lax.rem(z + k, NZ))) for k in range(1, NZ)]
    cpeer = at(core=oc)
    opeer = (dp, 1 - xl)

    def along(c):
        there = lax.rem(dp + NDP + c, NDP)
        return there, lax.rem(xl + xh + lax.div(there, 2 * NY * NZ), 2)

    after = [along(1), along(2)]
    side = along(2 * core - 1)

    barrier = pltpu.get_barrier_semaphore()
    near = [ypeer[k - 1][1] for k in (1, 2, 6, 7)] + [zpeer[k - 1][1] for k in (1, 2, 3, 9, 10, 11)]
    peers = [along(-2), after[1], side, cpeer] + [d for _, d in xpeer] + near
    for d in peers:
        pl.semaphore_signal(barrier, inc=1, device_id=d, device_id_type=MESH)

    def remote(src, dst, s, r, d):
        return pltpu.make_async_remote_copy(
            src_ref=src, dst_ref=dst, send_sem=s, recv_sem=r, device_id=d, device_id_type=MESH
        )

    sent = []

    def send(*args):
        c = remote(*args)
        c.start()
        sent.append(c)
        return c

    def embed(resid, hidden, weight, emb_out, dir_out, len_out):
        edge = dot(hidden[...], weight[...]) + resid[:, BLK:].astype(F32)
        body = resid[:, :BLK].astype(F32)
        square = jnp.sum(body * body, axis=1, keepdims=True) + jnp.sum(
            edge * edge, axis=1, keepdims=True
        )
        length = jnp.sqrt(square + 1e-06)
        inverse = 1.0 / length
        emb_out[:, :BLK] = (body * inverse).astype(BF16)
        direction = edge * inverse
        emb_out[:, BLK:] = direction.astype(BF16)
        dir_out[...] = direction
        len_out[...] = jnp.broadcast_to(inverse, len_out.shape)

    for n in range(3):
        loads[n].wait()
    embed(ir, ih, ew.at[0], emb, idir, ilen)
    pl.semaphore_wait(barrier, len(peers))

    far_copy = remote(emb, vis.at[1], vs_sem.at[1], vr_sem.at[1], along(-2))
    near_copy = remote(emb, vis.at[0], vs_sem.at[0], vr_sem.at[0], cpeer)
    onward = remote(vis.at[1], vis.at[0], vs_sem.at[0], vr_sem.at[0], cpeer)

    @pl.when(core == 0)
    def _():
        far_copy.start()

    @pl.when(core == 1)
    def _():
        near_copy.start()

    for d in near:
        pl.semaphore_signal(ready, inc=1, device_id=d, device_id_type=MESH)
    for c in loads[6:]:
        c.start()
    for n in range(3, 6):
        loads[n].wait()
    embed(tr, th, ew.at[1], temb, tdir, tlen)

    def pair(view, diagonal):
        images = view[...]
        sims = dot(temb[...], images, (1, 1))
        probs = 1.0 / (1.0 + jnp.exp(2.0 - 10.0 * sims))
        if diagonal:
            text = lax.broadcasted_iota(jnp.int32, sims.shape, 0)
            image = lax.broadcasted_iota(jnp.int32, sims.shape, 1) + xl * ROWS
            probs = probs - (text == image).astype(F32)
        weights = probs.astype(BF16)
        radial = weights.astype(F32) * sims
        txt_edge = dot(weights, images[:, BLK:])
        txt_radial = jnp.sum(radial, axis=1, keepdims=True)
        img_edge = dot(weights, temb[:, BLK:], (0, 0))
        img_radial = jnp.sum(radial, axis=0, keepdims=True)
        return img_edge, img_radial, txt_edge - tdir[...] * txt_radial

    own_edge, own_radial, txt_total = pair(emb, True)
    back[2, :ROWS] = own_edge
    back[2, ROWS:] = jnp.broadcast_to(own_radial, (8, EDGE))
    tout[...] = txt_total
    iht[...] = ih[...].T
    tht[...] = th[rows_at(xl * ROWS, ROWS)].T

    @pl.when(core == 1)
    def _():
        far_copy.start()

    @pl.when(core == 0)
    def _():
        far_copy.wait_recv()
        onward.start()

    for slot in range(2):
        if slot == 0:
            near_copy.wait_recv()
        else:
            @pl.when(core == 1)
            def _():
                far_copy.wait_recv()

        edge, radial, txt_edge = pair(vis.at[slot], False)
        back[slot, :ROWS] = edge
        back[slot, ROWS:] = jnp.broadcast_to(radial, (8, EDGE))
        send(back.at[slot], back_in.at[slot], bs_sem.at[slot], br_sem.at[slot], after[slot])
        tout[...] = tout[...] + txt_edge
    sent.append(far_copy)
    sent.append(near_copy)
    send(tout.at[rows_at((1 - xl) * ROWS, ROWS)], tin, ts_sem, tr_sem, opeer)

    mine = rows_at(core * 512, 512)
    theirs = rows_at(oc * 512, 512)
    for slot in range(2):
        remote(
            back.at[slot], back_in.at[slot], bs_sem.at[slot], br_sem.at[slot], cpeer
        ).wait_recv()
    total = back[2] + back_in[0] + back_in[1]
    radial = jnp.broadcast_to(total[ROWS:ROWS + 1], (ROWS, EDGE)).T
    dz = ((total[:ROWS] - idir[...] * radial) * ilen[...]).astype(BF16)
    p[0, theirs] = dot(iht[theirs], dz)
    ccopies = [send(p.at[0, theirs], cbuf.at[0], cs_sem.at[0], cr_sem.at[0], cpeer)]
    p[0, mine] = dot(iht[mine], dz)
    remote(tin, tin, ts_sem, tr_sem, opeer).wait_recv()
    own = rows_at(xl * ROWS, ROWS)
    dz = ((tout[own] + tin[...]) * tlen[own]).astype(BF16)
    p[1, theirs] = dot(tht[theirs], dz)
    ccopies.append(send(p.at[1, theirs], cbuf.at[1], cs_sem.at[1], cr_sem.at[1], cpeer))
    p[1, mine] = dot(tht[mine], dz)

    for t in range(2):
        ccopies[t].wait_recv()
        acc1[t] = (p[t, mine] + cbuf[t]).reshape(NY, 2, 32, EDGE)
        for h in (1, 0):
            k = lax.rem(2 * h + t + 4 - x, 4)
            slot = lax.max(k - 1, 0)

            @pl.when(k > 0)
            def _():
                xsend[slot] = acc1[t, :, h].astype(BF16)
                remote(
                    xsend.at[slot], xbuf.at[slot], xs_sem.at[slot], xr_sem.at[slot],
                    at(xh=h, xl=t),
                ).start()

    loads[6].wait()

    @pl.loop(0, 8)
    def _(i):
        r = rows_at(i * 128, 128)
        value = left[r]
        high = value.astype(BF16)
        lhi[r] = high
        llo[r] = (value - high.astype(F32)).astype(BF16)

    total = acc1[xl, :, xh]
    for k in range(3):
        c = remote(xsend.at[k], xbuf.at[k], xs_sem.at[k], xr_sem.at[k], cpeer)
        c.wait_recv()
        sent.append(c)
        total = total + xbuf[k].astype(F32)
    acc2[...] = total
    ysend[...] = total.astype(BF16)
    pl.semaphore_wait(ready, len(near))
    ycopies = []
    for k in YORDER:
        py, d = ypeer[k - 1]
        ycopies.append(send(
            ysend.at[py], ybuf.at[k - 1], ys_sem.at[k - 1], yr_sem.at[k - 1], d
        ))
    part = acc2[y]
    for c in ycopies:
        c.wait_recv()
    for k in range(NY - 1):
        part = part + ybuf[k].astype(F32)
    zbuf[z] = part.astype(BF16)
    for k in ZORDER:
        send(zbuf.at[z], zbuf.at[z], zs_sem.at[k - 1], zr_sem.at[k - 1], zpeer[k - 1][1])
    loads[7].wait()
    loads[8].wait()
    value = right[...]
    high = value.astype(BF16)
    rboth = jnp.concatenate([high, (value - high.astype(F32)).astype(BF16)], axis=1)
    for k in ZORDER:
        src = lax.rem(z + NZ - k, NZ)
        remote(zbuf.at[src], zbuf.at[src], zs_sem.at[k - 1], zr_sem.at[k - 1], cpeer).wait_recv()
    part = zbuf[0].astype(F32)
    for k in range(1, NZ):
        part = part + zbuf[k].astype(F32)
    at_y = core * NY + y
    gbuf[at_y, xh] = part.astype(BF16)
    own = gbuf.at[at_y, xh]
    offsets = [(k, h) for k in (4, 3, 5, 2, 6, 1, 7, 0) for h in (1, 0)][:-1]
    for n, (k, h) in enumerate(offsets):
        d = at(y=lax.rem(y + k, NY), xh=lax.rem(xh + h, 2))
        send(own, own, gs_sem.at[n], gr_sem.at[n], d)
    for n, (k, h) in enumerate(offsets):
        came = gbuf.at[core * NY + lax.rem(y + NY - k, NY), lax.rem(xh + h, 2)]
        remote(came, came, gs_sem.at[n], gr_sem.at[n], cpeer).wait_recv()
    own = gbuf.at[pl.ds(core * NY, NY)]
    send(own, own, ks_sem, kr_sem, cpeer)

    def half(c, first):
        g = gbuf[pl.ds(c * NY, NY)].reshape(512, EDGE)
        r = rows_at(c * 512, 512)
        v = dot(g, rboth)
        v = v[:, :EDGE] + v[:, EDGE:]
        high = v.astype(BF16)
        both = jnp.concatenate([high, (v - high.astype(F32)).astype(BF16)], axis=1)

        def body(i, total):
            o = rows_at(i * 256, 256)
            v = dot(lhi[o, r], both)
            v = v[:, :EDGE] + v[:, EDGE:] + dot(llo[o, r], high)
            if not first:
                v = v + cond[o]
            cond[o] = v
            return total if first else total + jnp.sum(v * v)

        csum = lax.fori_loop(0, 4, body, jnp.float32(0.0))
        g = g.astype(F32)
        square = g * g
        return jnp.sum(square / (acc[r] + square)), csum

    gsum, _ = half(core, True)
    other = gbuf.at[pl.ds(oc * NY, NY)]
    remote(other, other, ks_sem, kr_sem, cpeer).wait_recv()
    more, csum = half(oc, False)
    factor = jnp.sqrt(gsum + more) / jnp.sqrt(csum + 1e-06)
    out_ref[...] = cond[...] * factor
    for c in sent:
        c.wait_send()


def on_device(*args):
    dma = pltpu.SemaphoreType.DMA
    hbm = pl.BlockSpec(memory_space=pl.ANY)

    def f32(*shape):
        return pltpu.VMEM(shape, F32)

    def bf16(*shape):
        return pltpu.VMEM(shape, BF16)

    args = args[:5] + tuple(a.reshape(a.shape[1:]) for a in args[5:])
    out = pl.pallas_call(
        kernel,
        out_shape=jax.ShapeDtypeStruct((BLK, EDGE), F32),
        in_specs=[hbm] * 8,
        out_specs=pl.BlockSpec(memory_space=pltpu.VMEM),
        scratch_shapes=[
            bf16(ROWS, D), bf16(ROWS, BLK), bf16(TXT, D), bf16(TXT, BLK), bf16(2, BLK, EDGE),
            f32(BLK, BLK), f32(EDGE, EDGE), f32(BLK, EDGE),
            bf16(ROWS, D), f32(ROWS, EDGE), f32(ROWS, EDGE),
            bf16(TXT, D), f32(TXT, EDGE), f32(TXT, EDGE),
            bf16(2, ROWS, D), f32(3, ROWS + 8, EDGE), f32(2, ROWS + 8, EDGE),
            f32(TXT, EDGE), f32(ROWS, EDGE), bf16(BLK, ROWS), bf16(BLK, ROWS),
            bf16(BLK, BLK), bf16(BLK, BLK),
            f32(2, BLK, EDGE), f32(2, 512, EDGE), f32(2, NY, 2, 32, EDGE),
            bf16(3, NY, 32, EDGE), bf16(3, NY, 32, EDGE), f32(NY, 32, EDGE),
            bf16(NY, 32, EDGE), bf16(NY - 1, 32, EDGE), bf16(NZ, 32, EDGE),
            bf16(2 * NY, 2, 32, EDGE), f32(BLK, EDGE), pltpu.SemaphoreType.REGULAR,
            dma((9,)), dma((2,)), dma((2,)), dma((2,)), dma((2,)), dma, dma,
            dma((2,)), dma((2,)), dma((3,)), dma((3,)), dma((NY - 1,)), dma((NY - 1,)),
            dma((NZ - 1,)), dma((NZ - 1,)), dma((2 * NY - 1,)), dma((2 * NY - 1,)),
            dma, dma,
        ],
        compiler_params=pltpu.CompilerParams(
            collective_id=0, has_side_effects=True, vmem_limit_bytes=60 << 20
        ),
    )(*args)
    return out[None]


def solution(mesh):
    placed = (
        P(("dp", "opt"), None),
        P(("dp", "opt"), None),
        P("dp", None),
        P("dp", None),
        P(),
        P("opt", None, None),
        P("opt", None, None),
        P("opt", None, None),
    )
    return jax.shard_map(
        on_device, mesh=mesh, in_specs=placed, out_specs=P("opt", None, None), check_vma=False
    )
```

```python
import jax
import jax.numpy as jnp
from jax import lax
from jax.experimental import pallas as pl
from jax.experimental.pallas import tpu as pltpu
from jax.sharding import PartitionSpec as P

NX, NY, NZ, NDP = 2, 8, 12, 384
D, BLK, EDGE = 1152, 1024, 128
ROWS, TXT = 128, 256
MESH = pl.DeviceIdType.MESH
F32 = jnp.float32
BF16 = jnp.bfloat16
YORDER = (4, 3, 5, 2, 6, 1, 7)
ZORDER = (6, 5, 7, 4, 8, 3, 9, 2, 10, 1, 11)


def rows_at(start, size):
    return pl.ds(pl.multiple_of(start, size), size)


def dot(a, b, dims=(1, 0)):
    return lax.dot_general(
        a, b, (((dims[0],), (dims[1],)), ((), ())), preferred_element_type=F32
    )


def kernel(
    img_resid, img_hidden, txt_resid, txt_hidden, edge_weight, left_hbm, right_hbm, acc_hbm,
    out_ref,
    ir, ih, tr, th, ew, left, right, acc,
    emb, idir, ilen, temb, tdir, tlen, vis, back, back_in, iedge, iradial, tout, tin,
    iht, tht, lhi, llo,
    p, cbuf, acc1, xsend, xbuf, acc2, ysend, ybuf, zbuf, gbuf, cond, ready,
    load_sem, es_sem, er_sem, vs_sem, vr_sem, bs_sem, br_sem, ts_sem, tr_sem,
    cs_sem, cr_sem, xs_sem, xr_sem, ys_sem, yr_sem, zs_sem, zr_sem,
    gs_sem, gr_sem, ks_sem, kr_sem,
):
    dp = lax.axis_index("dp")
    xl = lax.axis_index("opt")
    core = lax.rem(dp, 2)
    y = lax.rem(lax.div(dp, 2), NY)
    z = lax.rem(lax.div(dp, 2 * NY), NZ)
    xh = lax.div(dp, 2 * NY * NZ)
    oc = 1 - core

    def at(xh=xh, z=z, y=y, core=core, xl=xl):
        return (((xh * NZ + z) * NY + y) * 2 + core, xl)

    half_rows = rows_at(xl * ROWS, ROWS)
    other_rows = rows_at((1 - xl) * ROWS, ROWS)
    loads = []
    for n, (src, dst) in enumerate([
        (txt_hidden.at[half_rows], th), (edge_weight.at[1], ew.at[1]),
        (txt_resid.at[half_rows], tr),
        (img_hidden, ih), (edge_weight.at[0], ew.at[0]), (img_resid, ir),
        (left_hbm, left), (right_hbm, right), (acc_hbm, acc),
    ]):
        loads.append(pltpu.make_async_copy(src, dst, load_sem.at[n]))
    for c in loads[:6]:
        c.start()

    x = xh * 2 + xl
    xpeer = []
    for k in range(1, 4):
        px = lax.rem(x + k, 4)
        xpeer.append((px, at(xh=lax.div(px, 2), xl=lax.rem(px, 2))))
    ypeer = [(lax.rem(y + k, NY), at(y=lax.rem(y + k, NY))) for k in range(1, NY)]
    zpeer = [(lax.rem(z + k, NZ), at(z=lax.rem(z + k, NZ))) for k in range(1, NZ)]
    cpeer = at(core=oc)
    opeer = (dp, 1 - xl)

    def along(c):
        there = lax.rem(dp + NDP + c, NDP)
        return there, lax.rem(xl + xh + lax.div(there, 2 * NY * NZ), 2)

    before = [along(-1), along(-2)]
    side = along(2 * core - 1)

    barrier = pltpu.get_barrier_semaphore()
    near = [ypeer[k - 1][1] for k in (1, 2, 6, 7)] + [zpeer[k - 1][1] for k in (1, 2, 3, 9, 10, 11)]
    peers = [along(2), before[1], side, cpeer] + [d for _, d in xpeer] + near
    for d in peers:
        pl.semaphore_signal(barrier, inc=1, device_id=d, device_id_type=MESH)

    def remote(src, dst, s, r, d):
        return pltpu.make_async_remote_copy(
            src_ref=src, dst_ref=dst, send_sem=s, recv_sem=r, device_id=d, device_id_type=MESH
        )

    sent = []

    def send(*args):
        c = remote(*args)
        c.start()
        sent.append(c)
        return c

    def embed(resid, hidden, weight, emb_out, dir_out, len_out):
        edge = dot(hidden[...], weight[...]) + resid[:, BLK:].astype(F32)
        body = resid[:, :BLK].astype(F32)
        square = jnp.sum(body * body, axis=1, keepdims=True) + jnp.sum(
            edge * edge, axis=1, keepdims=True
        )
        length = jnp.sqrt(square + 1e-06)
        inverse = 1.0 / length
        emb_out[:, :BLK] = (body * inverse).astype(BF16)
        direction = edge * inverse
        emb_out[:, BLK:] = direction.astype(BF16)
        dir_out[...] = direction
        len_out[...] = jnp.broadcast_to(inverse, len_out.shape)

    for n in range(3):
        loads[n].wait()
    embed(tr, th, ew.at[1], temb, tdir, tlen)
    pl.semaphore_wait(barrier, len(peers))

    far_copy = remote(temb, vis.at[1], vs_sem.at[1], vr_sem.at[1], along(2))
    near_copy = remote(temb, vis.at[0], vs_sem.at[0], vr_sem.at[0], cpeer)
    onward = remote(vis.at[1], vis.at[0], vs_sem.at[0], vr_sem.at[0], cpeer)

    @pl.when(core == 1)
    def _():
        far_copy.start()

    @pl.when(core == 0)
    def _():
        near_copy.start()

    for d in near:
        pl.semaphore_signal(ready, inc=1, device_id=d, device_id_type=MESH)
    for c in loads[6:]:
        c.start()
    for n in range(3, 6):
        loads[n].wait()
    embed(ir, ih, ew.at[0], emb.at[half_rows], idir, ilen)
    send(emb.at[half_rows], emb.at[half_rows], es_sem, er_sem, opeer)

    @pl.when(core == 0)
    def _():
        far_copy.start()

    iht[...] = ih[...].T
    tht[...] = th[...].T

    def pair(view, diagonal):
        texts = view[...]
        sims = dot(emb[...], texts, (1, 1))
        probs = 1.0 / (1.0 + jnp.exp(2.0 - 10.0 * sims))
        if diagonal:
            image = lax.broadcasted_iota(jnp.int32, sims.shape, 0)
            text = lax.broadcasted_iota(jnp.int32, sims.shape, 1) + xl * ROWS
            probs = probs - (text == image).astype(F32)
        weights = probs.astype(BF16)
        radial = weights.astype(F32) * sims
        img_edge = dot(weights, texts[:, BLK:])
        img_radial = jnp.sum(radial, axis=1, keepdims=True)
        txt_edge = dot(weights, emb[:, BLK:], (0, 0))
        txt_radial = jnp.sum(radial, axis=0, keepdims=True)
        return txt_edge, txt_radial, img_edge, jnp.broadcast_to(img_radial, (TXT, EDGE))

    @pl.when(core == 1)
    def _():
        far_copy.wait_recv()
        onward.start()

    remote(emb.at[other_rows], emb.at[other_rows], es_sem, er_sem, opeer).wait_recv()
    own_edge, own_radial, img_edge, img_radial = pair(temb, True)
    back[2, :ROWS] = own_edge
    back[2, ROWS:] = jnp.broadcast_to(own_radial, (8, EDGE))
    iedge[...] = img_edge
    iradial[...] = img_radial

    for slot in range(2):
        if slot == 0:
            near_copy.wait_recv()
        else:
            @pl.when(core == 0)
            def _():
                far_copy.wait_recv()

        edge, radial, img_edge, img_radial = pair(vis.at[slot], False)
        back[slot, :ROWS] = edge
        back[slot, ROWS:] = jnp.broadcast_to(radial, (8, EDGE))
        send(back.at[slot], back_in.at[slot], bs_sem.at[slot], br_sem.at[slot], before[slot])
        iedge[...] = iedge[...] + img_edge
        iradial[...] = iradial[...] + img_radial
    sent.append(far_copy)
    sent.append(near_copy)
    tout[:ROWS] = iedge[other_rows]
    tout[ROWS:] = iradial[other_rows].T[:8]
    send(tout, tin, ts_sem, tr_sem, opeer)

    mine = rows_at(core * 512, 512)
    theirs = rows_at(oc * 512, 512)

    def edge_dz(edge, radial, direction, inverse):
        return ((edge - direction[...] * radial) * inverse[...]).astype(BF16)

    def across(row):
        return jnp.broadcast_to(row, (ROWS, EDGE)).T

    remote(tin, tin, ts_sem, tr_sem, opeer).wait_recv()
    radial = iradial[half_rows] + across(tin[ROWS:ROWS + 1])
    dz = edge_dz(iedge[half_rows] + tin[:ROWS], radial, idir, ilen)
    p[0, theirs] = dot(iht[theirs], dz)
    ccopies = [send(p.at[0, theirs], cbuf.at[0], cs_sem.at[0], cr_sem.at[0], cpeer)]
    p[0, mine] = dot(iht[mine], dz)
    for slot in range(2):
        remote(
            back.at[slot], back_in.at[slot], bs_sem.at[slot], br_sem.at[slot], cpeer
        ).wait_recv()
    total = back[2] + back_in[0] + back_in[1]
    dz = edge_dz(total[:ROWS], across(total[ROWS:ROWS + 1]), tdir, tlen)
    p[1, theirs] = dot(tht[theirs], dz)
    ccopies.append(send(p.at[1, theirs], cbuf.at[1], cs_sem.at[1], cr_sem.at[1], cpeer))
    p[1, mine] = dot(tht[mine], dz)

    for t in range(2):
        ccopies[t].wait_recv()
        acc1[t] = (p[t, mine] + cbuf[t]).reshape(NY, 2, 32, EDGE)
        for h in (1, 0):
            k = lax.rem(2 * h + t + 4 - x, 4)
            slot = lax.max(k - 1, 0)

            @pl.when(k > 0)
            def _():
                xsend[slot] = acc1[t, :, h].astype(BF16)
                remote(
                    xsend.at[slot], xbuf.at[slot], xs_sem.at[slot], xr_sem.at[slot],
                    at(xh=h, xl=t),
                ).start()

    loads[6].wait()

    @pl.loop(0, 8)
    def _(i):
        r = rows_at(i * 128, 128)
        value = left[r]
        high = value.astype(BF16)
        lhi[r] = high
        llo[r] = (value - high.astype(F32)).astype(BF16)

    total = acc1[xl, :, xh]
    for k in range(3):
        c = remote(xsend.at[k], xbuf.at[k], xs_sem.at[k], xr_sem.at[k], cpeer)
        c.wait_recv()
        sent.append(c)
        total = total + xbuf[k].astype(F32)
    acc2[...] = total
    ysend[...] = total.astype(BF16)
    pl.semaphore_wait(ready, len(near))
    ycopies = []
    for k in YORDER:
        py, d = ypeer[k - 1]
        ycopies.append(send(
            ysend.at[py], ybuf.at[k - 1], ys_sem.at[k - 1], yr_sem.at[k - 1], d
        ))
    part = acc2[y]
    for c in ycopies:
        c.wait_recv()
    for k in range(NY - 1):
        part = part + ybuf[k].astype(F32)
    zbuf[z] = part.astype(BF16)
    for k in ZORDER:
        send(zbuf.at[z], zbuf.at[z], zs_sem.at[k - 1], zr_sem.at[k - 1], zpeer[k - 1][1])
    loads[7].wait()
    loads[8].wait()
    value = right[...]
    high = value.astype(BF16)
    rboth = jnp.concatenate([high, (value - high.astype(F32)).astype(BF16)], axis=1)
    for k in ZORDER:
        src = lax.rem(z + NZ - k, NZ)
        remote(zbuf.at[src], zbuf.at[src], zs_sem.at[k - 1], zr_sem.at[k - 1], cpeer).wait_recv()
    part = zbuf[0].astype(F32)
    for k in range(1, NZ):
        part = part + zbuf[k].astype(F32)
    at_y = core * NY + y
    gbuf[at_y, xh] = part.astype(BF16)
    own = gbuf.at[at_y, xh]
    offsets = [(k, h) for k in (4, 3, 5, 2, 6, 1, 7, 0) for h in (1, 0)][:-1]
    for n, (k, h) in enumerate(offsets):
        d = at(y=lax.rem(y + k, NY), xh=lax.rem(xh + h, 2))
        send(own, own, gs_sem.at[n], gr_sem.at[n], d)
    for n, (k, h) in enumerate(offsets):
        came = gbuf.at[core * NY + lax.rem(y + NY - k, NY), lax.rem(xh + h, 2)]
        remote(came, came, gs_sem.at[n], gr_sem.at[n], cpeer).wait_recv()
    own = gbuf.at[pl.ds(core * NY, NY)]
    send(own, own, ks_sem, kr_sem, cpeer)

    def half(c, first):
        g = gbuf[pl.ds(c * NY, NY)].reshape(512, EDGE)
        r = rows_at(c * 512, 512)
        v = dot(g, rboth)
        v = v[:, :EDGE] + v[:, EDGE:]
        high = v.astype(BF16)
        both = jnp.concatenate([high, (v - high.astype(F32)).astype(BF16)], axis=1)

        def body(i, total):
            o = rows_at(i * 256, 256)
            v = dot(lhi[o, r], both)
            v = v[:, :EDGE] + v[:, EDGE:] + dot(llo[o, r], high)
            if not first:
                v = v + cond[o]
            cond[o] = v
            return total if first else total + jnp.sum(v * v)

        csum = lax.fori_loop(0, 4, body, jnp.float32(0.0))
        g = g.astype(F32)
        square = g * g
        return jnp.sum(square / (acc[r] + square)), csum

    gsum, _ = half(core, True)
    other = gbuf.at[pl.ds(oc * NY, NY)]
    remote(other, other, ks_sem, kr_sem, cpeer).wait_recv()
    more, csum = half(oc, False)
    factor = jnp.sqrt(gsum + more) / jnp.sqrt(csum + 1e-06)
    out_ref[...] = cond[...] * factor
    for c in sent:
        c.wait_send()


def on_device(*args):
    dma = pltpu.SemaphoreType.DMA
    hbm = pl.BlockSpec(memory_space=pl.ANY)

    def f32(*shape):
        return pltpu.VMEM(shape, F32)

    def bf16(*shape):
        return pltpu.VMEM(shape, BF16)

    args = args[:5] + tuple(a.reshape(a.shape[1:]) for a in args[5:])
    out = pl.pallas_call(
        kernel,
        out_shape=jax.ShapeDtypeStruct((BLK, EDGE), F32),
        in_specs=[hbm] * 8,
        out_specs=pl.BlockSpec(memory_space=pltpu.VMEM),
        scratch_shapes=[
            bf16(ROWS, D), bf16(ROWS, BLK), bf16(ROWS, D), bf16(ROWS, BLK), bf16(2, BLK, EDGE),
            f32(BLK, BLK), f32(EDGE, EDGE), f32(BLK, EDGE),
            bf16(TXT, D), f32(ROWS, EDGE), f32(ROWS, EDGE),
            bf16(ROWS, D), f32(ROWS, EDGE), f32(ROWS, EDGE),
            bf16(2, ROWS, D), f32(3, ROWS + 8, EDGE), f32(2, ROWS + 8, EDGE),
            f32(TXT, EDGE), f32(TXT, EDGE), f32(ROWS + 8, EDGE), f32(ROWS + 8, EDGE),
            bf16(BLK, ROWS), bf16(BLK, ROWS),
            bf16(BLK, BLK), bf16(BLK, BLK),
            f32(2, BLK, EDGE), f32(2, 512, EDGE), f32(2, NY, 2, 32, EDGE),
            bf16(3, NY, 32, EDGE), bf16(3, NY, 32, EDGE), f32(NY, 32, EDGE),
            bf16(NY, 32, EDGE), bf16(NY - 1, 32, EDGE), bf16(NZ, 32, EDGE),
            bf16(2 * NY, 2, 32, EDGE), f32(BLK, EDGE), pltpu.SemaphoreType.REGULAR,
            dma((9,)), dma, dma, dma((2,)), dma((2,)), dma((2,)), dma((2,)), dma, dma,
            dma((2,)), dma((2,)), dma((3,)), dma((3,)), dma((NY - 1,)), dma((NY - 1,)),
            dma((NZ - 1,)), dma((NZ - 1,)), dma((2 * NY - 1,)), dma((2 * NY - 1,)),
            dma, dma,
        ],
        compiler_params=pltpu.CompilerParams(
            collective_id=0, has_side_effects=True, vmem_limit_bytes=60 << 20
        ),
    )(*args)
    return out[None]


def solution(mesh):
    placed = (
        P(("dp", "opt"), None),
        P(("dp", "opt"), None),
        P("dp", None),
        P("dp", None),
        P(),
        P("opt", None, None),
        P("opt", None, None),
        P("opt", None, None),
    )
    return jax.shard_map(
        on_device, mesh=mesh, in_specs=placed, out_specs=P("opt", None, None), check_vma=False
    )
```

```python
import jax
import jax.numpy as jnp
from jax import lax
from jax.experimental import pallas as pl
from jax.experimental.pallas import tpu as pltpu
from jax.sharding import PartitionSpec as P

NX, NY, NZ, NDP = 2, 8, 12, 384
D, BLK, EDGE = 1152, 1024, 128
ROWS, TXT = 128, 256
MESH = pl.DeviceIdType.MESH
F32 = jnp.float32
BF16 = jnp.bfloat16
YORDER = (4, 3, 5, 2, 6, 1, 7)
ZORDER = (6, 5, 7, 4, 8, 3, 9, 2, 10, 1, 11)


def rows_at(start, size):
    return pl.ds(pl.multiple_of(start, size), size)


def dot(a, b, dims=(1, 0)):
    return lax.dot_general(
        a, b, (((dims[0],), (dims[1],)), ((), ())), preferred_element_type=F32
    )


def kernel(
    img_resid, img_hidden, txt_resid, txt_hidden, edge_weight, left_hbm, right_hbm, acc_hbm,
    out_ref,
    ir, ih, tr, th, ew, left, right, acc,
    emb, idir, ilen, temb, tdir, tlen, vis, back, back_in, iedge, iradial, tout, tin,
    iht, tht, lhi, llo,
    p, csend, cbuf, acc1, xsend, xbuf, acc2, ysend, ybuf, zbuf, gbuf, cond, ready, go,
    load_sem, es_sem, er_sem, vs_sem, vr_sem, bs_sem, br_sem, ts_sem, tr_sem,
    cs_sem, cr_sem, xs_sem, xr_sem, ys_sem, yr_sem, zs_sem, zr_sem,
    gs_sem, gr_sem, ks_sem, kr_sem,
):
    dp = lax.axis_index("dp")
    xl = lax.axis_index("opt")
    core = lax.rem(dp, 2)
    y = lax.rem(lax.div(dp, 2), NY)
    z = lax.rem(lax.div(dp, 2 * NY), NZ)
    xh = lax.div(dp, 2 * NY * NZ)
    oc = 1 - core

    def at(xh=xh, z=z, y=y, core=core, xl=xl):
        return (((xh * NZ + z) * NY + y) * 2 + core, xl)

    half_rows = rows_at(xl * ROWS, ROWS)
    other_rows = rows_at((1 - xl) * ROWS, ROWS)
    loads = []
    for n, (src, dst) in enumerate([
        (txt_hidden.at[half_rows], th), (edge_weight.at[1], ew.at[1]),
        (txt_resid.at[half_rows], tr),
        (img_hidden, ih), (edge_weight.at[0], ew.at[0]), (img_resid, ir),
        (left_hbm, left), (right_hbm, right), (acc_hbm, acc),
    ]):
        loads.append(pltpu.make_async_copy(src, dst, load_sem.at[n]))
    for c in loads[:6]:
        c.start()

    x = xh * 2 + xl
    xpeer = []
    for k in range(1, 4):
        px = lax.rem(x + k, 4)
        xpeer.append((px, at(xh=lax.div(px, 2), xl=lax.rem(px, 2))))
    ypeer = [(lax.rem(y + k, NY), at(y=lax.rem(y + k, NY))) for k in range(1, NY)]
    zpeer = [(lax.rem(z + k, NZ), at(z=lax.rem(z + k, NZ))) for k in range(1, NZ)]
    cpeer = at(core=oc)
    opeer = (dp, 1 - xl)

    def along(c):
        there = lax.rem(dp + NDP + c, NDP)
        return there, lax.rem(xl + xh + lax.div(there, 2 * NY * NZ), 2)

    before = [along(-1), along(-2)]
    side = along(2 * core - 1)

    barrier = pltpu.get_barrier_semaphore()
    near = [ypeer[k - 1][1] for k in (1, 2, 6, 7)] + [zpeer[k - 1][1] for k in (1, 2, 3, 9, 10, 11)]
    peers = [along(2), before[1], side, cpeer] + [d for _, d in xpeer] + near
    for d in peers:
        pl.semaphore_signal(barrier, inc=1, device_id=d, device_id_type=MESH)

    def remote(src, dst, s, r, d):
        return pltpu.make_async_remote_copy(
            src_ref=src, dst_ref=dst, send_sem=s, recv_sem=r, device_id=d, device_id_type=MESH
        )

    sent = []

    def send(*args):
        c = remote(*args)
        c.start()
        sent.append(c)
        return c

    def embed(resid, hidden, weight, emb_out, dir_out, len_out):
        edge = dot(hidden[...], weight[...]) + resid[:, BLK:].astype(F32)
        body = resid[:, :BLK].astype(F32)
        square = jnp.sum(body * body, axis=1, keepdims=True) + jnp.sum(
            edge * edge, axis=1, keepdims=True
        )
        length = jnp.sqrt(square + 1e-06)
        inverse = 1.0 / length
        emb_out[:, :BLK] = (body * inverse).astype(BF16)
        direction = edge * inverse
        emb_out[:, BLK:] = direction.astype(BF16)
        dir_out[...] = direction
        len_out[...] = jnp.broadcast_to(inverse, len_out.shape)

    for n in range(3):
        loads[n].wait()
    embed(tr, th, ew.at[1], temb, tdir, tlen)
    pl.semaphore_wait(barrier, len(peers))

    far = [
        remote(temb.at[part], vis.at[1, part], vs_sem.at[n + 1], vr_sem.at[n + 1], along(2))
        for n, part in enumerate((pl.ds(0, 64), pl.ds(64, 64)))
    ]
    near_copy = remote(temb, vis.at[0], vs_sem.at[0], vr_sem.at[0], cpeer)
    onward = remote(vis.at[1], vis.at[0], vs_sem.at[0], vr_sem.at[0], cpeer)

    @pl.when(core == 1)
    def _():
        far[0].start()
        far[1].start()

    @pl.when(core == 0)
    def _():
        near_copy.start()

    for d in near:
        pl.semaphore_signal(ready, inc=1, device_id=d, device_id_type=MESH)
    for c in loads[6:]:
        c.start()
    for n in range(3, 6):
        loads[n].wait()
    embed(ir, ih, ew.at[0], emb.at[half_rows], idir, ilen)
    send(emb.at[half_rows], emb.at[half_rows], es_sem, er_sem, opeer)

    iht[...] = ih[...].T
    tht[...] = th[...].T

    @pl.when(core == 1)
    def _():
        far[0].wait_send()
        pl.semaphore_signal(go, inc=1, device_id=cpeer, device_id_type=MESH)

    @pl.when(core == 0)
    def _():
        pl.semaphore_wait(go, 1)
        far[0].start()
        far[1].start()

    def pair(view, diagonal):
        texts = view[...]
        sims = dot(emb[...], texts, (1, 1))
        probs = 1.0 / (1.0 + jnp.exp(2.0 - 10.0 * sims))
        if diagonal:
            image = lax.broadcasted_iota(jnp.int32, sims.shape, 0)
            text = lax.broadcasted_iota(jnp.int32, sims.shape, 1) + xl * ROWS
            probs = probs - (text == image).astype(F32)
        weights = probs.astype(BF16)
        radial = weights.astype(F32) * sims
        img_edge = dot(weights, texts[:, BLK:])
        img_radial = jnp.sum(radial, axis=1, keepdims=True)
        txt_edge = dot(weights, emb[:, BLK:], (0, 0))
        txt_radial = jnp.sum(radial, axis=0, keepdims=True)
        return txt_edge, txt_radial, img_edge, jnp.broadcast_to(img_radial, (TXT, EDGE))

    @pl.when(core == 1)
    def _():
        far[0].wait_recv()
        far[1].wait_recv()
        onward.start()

    remote(emb.at[other_rows], emb.at[other_rows], es_sem, er_sem, opeer).wait_recv()
    own_edge, own_radial, img_edge, img_radial = pair(temb, True)
    back[2, :ROWS] = own_edge
    back[2, ROWS:] = jnp.broadcast_to(own_radial, (8, EDGE))
    iedge[...] = img_edge
    iradial[...] = img_radial

    for slot in range(2):
        if slot == 0:
            near_copy.wait_recv()
        else:
            @pl.when(core == 0)
            def _():
                far[0].wait_recv()
                far[1].wait_recv()

        edge, radial, img_edge, img_radial = pair(vis.at[slot], False)
        back[slot, :ROWS] = edge
        back[slot, ROWS:] = jnp.broadcast_to(radial, (8, EDGE))
        send(back.at[slot], back_in.at[slot], bs_sem.at[slot], br_sem.at[slot], before[slot])
        iedge[...] = iedge[...] + img_edge
        iradial[...] = iradial[...] + img_radial
    sent.append(far[1])
    sent.append(near_copy)
    tout[:ROWS] = iedge[other_rows]
    tout[ROWS:] = iradial[other_rows].T[:8]
    send(tout, tin, ts_sem, tr_sem, opeer)

    mine = rows_at(core * 512, 512)
    theirs = rows_at(oc * 512, 512)

    def edge_dz(edge, radial, direction, inverse):
        return ((edge - direction[...] * radial) * inverse[...]).astype(BF16)

    def across(row):
        return jnp.broadcast_to(row, (ROWS, EDGE)).T

    remote(tin, tin, ts_sem, tr_sem, opeer).wait_recv()
    radial = iradial[half_rows] + across(tin[ROWS:ROWS + 1])
    dz = edge_dz(iedge[half_rows] + tin[:ROWS], radial, idir, ilen)
    csend[0] = dot(iht[theirs], dz).astype(BF16)
    ccopies = [send(csend.at[0], cbuf.at[0], cs_sem.at[0], cr_sem.at[0], cpeer)]
    p[0] = dot(iht[mine], dz)
    for slot in range(2):
        remote(
            back.at[slot], back_in.at[slot], bs_sem.at[slot], br_sem.at[slot], cpeer
        ).wait_recv()
    total = back[2] + back_in[0] + back_in[1]
    dz = edge_dz(total[:ROWS], across(total[ROWS:ROWS + 1]), tdir, tlen)
    csend[1] = dot(tht[theirs], dz).astype(BF16)
    ccopies.append(send(csend.at[1], cbuf.at[1], cs_sem.at[1], cr_sem.at[1], cpeer))
    p[1] = dot(tht[mine], dz)

    for t in range(2):
        ccopies[t].wait_recv()
        acc1[t] = (p[t] + cbuf[t].astype(F32)).reshape(NY, 2, 32, EDGE)
        for h in (1, 0):
            k = lax.rem(2 * h + t + 4 - x, 4)
            slot = lax.max(k - 1, 0)

            @pl.when(k > 0)
            def _():
                xsend[slot] = acc1[t, :, h].astype(BF16)
                remote(
                    xsend.at[slot], xbuf.at[slot], xs_sem.at[slot], xr_sem.at[slot],
                    at(xh=h, xl=t),
                ).start()

    loads[6].wait()

    @pl.loop(0, 8)
    def _(i):
        r = rows_at(i * 128, 128)
        value = left[r]
        high = value.astype(BF16)
        lhi[r] = high
        llo[r] = (value - high.astype(F32)).astype(BF16)

    total = acc1[xl, :, xh]
    for k in range(3):
        c = remote(xsend.at[k], xbuf.at[k], xs_sem.at[k], xr_sem.at[k], cpeer)
        c.wait_recv()
        sent.append(c)
        total = total + xbuf[k].astype(F32)
    acc2[...] = total
    ysend[...] = total.astype(BF16)
    pl.semaphore_wait(ready, len(near))
    ycopies = []
    for k in YORDER:
        py, d = ypeer[k - 1]
        ycopies.append(send(
            ysend.at[py], ybuf.at[k - 1], ys_sem.at[k - 1], yr_sem.at[k - 1], d
        ))
    part = acc2[y]
    for c in ycopies:
        c.wait_recv()
    for k in range(NY - 1):
        part = part + ybuf[k].astype(F32)
    zbuf[z] = part.astype(BF16)
    for k in ZORDER:
        send(zbuf.at[z], zbuf.at[z], zs_sem.at[k - 1], zr_sem.at[k - 1], zpeer[k - 1][1])
    loads[7].wait()
    loads[8].wait()
    value = right[...]
    high = value.astype(BF16)
    rboth = jnp.concatenate([high, (value - high.astype(F32)).astype(BF16)], axis=1)
    for k in ZORDER:
        src = lax.rem(z + NZ - k, NZ)
        remote(zbuf.at[src], zbuf.at[src], zs_sem.at[k - 1], zr_sem.at[k - 1], cpeer).wait_recv()
    part = zbuf[0].astype(F32)
    for k in range(1, NZ):
        part = part + zbuf[k].astype(F32)
    at_y = core * NY + y
    gbuf[at_y, xh] = part.astype(BF16)
    own = gbuf.at[at_y, xh]
    offsets = [(k, h) for k in (4, 3, 5, 2, 6, 1, 7, 0) for h in (1, 0)][:-1]
    for n, (k, h) in enumerate(offsets):
        d = at(y=lax.rem(y + k, NY), xh=lax.rem(xh + h, 2))
        send(own, own, gs_sem.at[n], gr_sem.at[n], d)
    for n, (k, h) in enumerate(offsets):
        came = gbuf.at[core * NY + lax.rem(y + NY - k, NY), lax.rem(xh + h, 2)]
        remote(came, came, gs_sem.at[n], gr_sem.at[n], cpeer).wait_recv()
    own = gbuf.at[pl.ds(core * NY, NY)]
    send(own, own, ks_sem, kr_sem, cpeer)

    def half(c, first):
        g = gbuf[pl.ds(c * NY, NY)].reshape(512, EDGE)
        r = rows_at(c * 512, 512)
        v = dot(g, rboth)
        v = v[:, :EDGE] + v[:, EDGE:]
        high = v.astype(BF16)
        both = jnp.concatenate([high, (v - high.astype(F32)).astype(BF16)], axis=1)

        def body(i, total):
            o = rows_at(i * 256, 256)
            v = dot(lhi[o, r], both)
            v = v[:, :EDGE] + v[:, EDGE:] + dot(llo[o, r], high)
            if not first:
                v = v + cond[o]
            cond[o] = v
            return total if first else total + jnp.sum(v * v)

        csum = lax.fori_loop(0, 4, body, jnp.float32(0.0))
        g = g.astype(F32)
        square = g * g
        return jnp.sum(square / (acc[r] + square)), csum

    gsum, _ = half(core, True)
    other = gbuf.at[pl.ds(oc * NY, NY)]
    remote(other, other, ks_sem, kr_sem, cpeer).wait_recv()
    more, csum = half(oc, False)
    factor = jnp.sqrt(gsum + more) / jnp.sqrt(csum + 1e-06)
    out_ref[...] = cond[...] * factor
    for c in sent:
        c.wait_send()

    @pl.when(core == 0)
    def _():
        far[0].wait_send()


def on_device(*args):
    dma = pltpu.SemaphoreType.DMA
    hbm = pl.BlockSpec(memory_space=pl.ANY)

    def f32(*shape):
        return pltpu.VMEM(shape, F32)

    def bf16(*shape):
        return pltpu.VMEM(shape, BF16)

    args = args[:5] + tuple(a.reshape(a.shape[1:]) for a in args[5:])
    out = pl.pallas_call(
        kernel,
        out_shape=jax.ShapeDtypeStruct((BLK, EDGE), F32),
        in_specs=[hbm] * 8,
        out_specs=pl.BlockSpec(memory_space=pltpu.VMEM),
        scratch_shapes=[
            bf16(ROWS, D), bf16(ROWS, BLK), bf16(ROWS, D), bf16(ROWS, BLK), bf16(2, BLK, EDGE),
            f32(BLK, BLK), f32(EDGE, EDGE), f32(BLK, EDGE),
            bf16(TXT, D), f32(ROWS, EDGE), f32(ROWS, EDGE),
            bf16(ROWS, D), f32(ROWS, EDGE), f32(ROWS, EDGE),
            bf16(2, ROWS, D), f32(3, ROWS + 8, EDGE), f32(2, ROWS + 8, EDGE),
            f32(TXT, EDGE), f32(TXT, EDGE), f32(ROWS + 8, EDGE), f32(ROWS + 8, EDGE),
            bf16(BLK, ROWS), bf16(BLK, ROWS),
            bf16(BLK, BLK), bf16(BLK, BLK),
            f32(2, 512, EDGE), bf16(2, 512, EDGE), bf16(2, 512, EDGE), f32(2, NY, 2, 32, EDGE),
            bf16(3, NY, 32, EDGE), bf16(3, NY, 32, EDGE), f32(NY, 32, EDGE),
            bf16(NY, 32, EDGE), bf16(NY - 1, 32, EDGE), bf16(NZ, 32, EDGE),
            bf16(2 * NY, 2, 32, EDGE), f32(BLK, EDGE),
            pltpu.SemaphoreType.REGULAR, pltpu.SemaphoreType.REGULAR,
            dma((9,)), dma, dma, dma((3,)), dma((3,)), dma((2,)), dma((2,)), dma, dma,
            dma((2,)), dma((2,)), dma((3,)), dma((3,)), dma((NY - 1,)), dma((NY - 1,)),
            dma((NZ - 1,)), dma((NZ - 1,)), dma((2 * NY - 1,)), dma((2 * NY - 1,)),
            dma, dma,
        ],
        compiler_params=pltpu.CompilerParams(
            collective_id=0, has_side_effects=True, vmem_limit_bytes=60 << 20
        ),
    )(*args)
    return out[None]


def solution(mesh):
    placed = (
        P(("dp", "opt"), None),
        P(("dp", "opt"), None),
        P("dp", None),
        P("dp", None),
        P(),
        P("opt", None, None),
        P("opt", None, None),
        P("opt", None, None),
    )
    return jax.shard_map(
        on_device, mesh=mesh, in_specs=placed, out_specs=P("opt", None, None), check_vma=False
    )
```

```python
import jax
import jax.numpy as jnp
from jax import lax
from jax.experimental import pallas as pl
from jax.experimental.pallas import tpu as pltpu
from jax.sharding import PartitionSpec as P

NX, NY, NZ, NDP = 2, 8, 12, 384
D, BLK, EDGE = 1152, 1024, 128
ROWS, TXT = 128, 256
MESH = pl.DeviceIdType.MESH
F32 = jnp.float32
BF16 = jnp.bfloat16
YORDER = (4, 3, 5, 2, 6, 1, 7)
ZORDER = (6, 5, 7, 4, 8, 3, 9, 2, 10, 1, 11)


def rows_at(start, size):
    return pl.ds(pl.multiple_of(start, size), size)


def dot(a, b, dims=(1, 0)):
    return lax.dot_general(
        a, b, (((dims[0],), (dims[1],)), ((), ())), preferred_element_type=F32
    )


def kernel(
    img_resid, img_hidden, txt_resid, txt_hidden, edge_weight, left_hbm, right_hbm, acc_hbm,
    out_ref,
    ir, ih, tr, th, ew, left, right, acc,
    emb, idir, ilen, temb, tdir, tlen, vis, back, back_in, iedge, iradial, tout, tin,
    iht, tht, lhi, llo,
    p, csend, cbuf, acc1, xsend, xbuf, ysend, ybuf, zbuf, gbuf, cond, ready, go,
    load_sem, es_sem, er_sem, vs_sem, vr_sem, bs_sem, br_sem, ts_sem, tr_sem,
    cs_sem, cr_sem, xs_sem, xr_sem, ys_sem, yr_sem, zs_sem, zr_sem,
    gs_sem, gr_sem, ks_sem, kr_sem,
):
    dp = lax.axis_index("dp")
    xl = lax.axis_index("opt")
    core = lax.rem(dp, 2)
    y = lax.rem(lax.div(dp, 2), NY)
    z = lax.rem(lax.div(dp, 2 * NY), NZ)
    xh = lax.div(dp, 2 * NY * NZ)
    oc = 1 - core

    def at(xh=xh, z=z, y=y, core=core, xl=xl):
        return (((xh * NZ + z) * NY + y) * 2 + core, xl)

    half_rows = rows_at(xl * ROWS, ROWS)
    other_rows = rows_at((1 - xl) * ROWS, ROWS)
    loads = []
    for n, (src, dst) in enumerate([
        (txt_hidden.at[half_rows], th), (edge_weight.at[1], ew.at[1]),
        (txt_resid.at[half_rows], tr),
        (img_hidden, ih), (edge_weight.at[0], ew.at[0]), (img_resid, ir),
        (left_hbm, left), (right_hbm, right), (acc_hbm, acc),
    ]):
        loads.append(pltpu.make_async_copy(src, dst, load_sem.at[n]))
    for c in loads[:6]:
        c.start()

    x = xh * 2 + xl
    xpeer = []
    for k in range(1, 4):
        px = lax.rem(x + k, 4)
        xpeer.append((px, at(xh=lax.div(px, 2), xl=lax.rem(px, 2))))
    ypeer = [(lax.rem(y + k, NY), at(y=lax.rem(y + k, NY))) for k in range(1, NY)]
    zpeer = [(lax.rem(z + k, NZ), at(z=lax.rem(z + k, NZ))) for k in range(1, NZ)]
    cpeer = at(core=oc)
    opeer = (dp, 1 - xl)

    def along(c):
        there = lax.rem(dp + NDP + c, NDP)
        return there, lax.rem(xl + xh + lax.div(there, 2 * NY * NZ), 2)

    before = [along(-1), along(-2)]
    side = along(2 * core - 1)

    barrier = pltpu.get_barrier_semaphore()
    near = [ypeer[k - 1][1] for k in (1, 2, 6, 7)] + [zpeer[k - 1][1] for k in (1, 2, 3, 9, 10, 11)]
    peers = [along(2), before[1], side, cpeer] + [d for _, d in xpeer] + near
    for d in peers:
        pl.semaphore_signal(barrier, inc=1, device_id=d, device_id_type=MESH)

    def remote(src, dst, s, r, d):
        return pltpu.make_async_remote_copy(
            src_ref=src, dst_ref=dst, send_sem=s, recv_sem=r, device_id=d, device_id_type=MESH
        )

    sent = []

    def send(*args):
        c = remote(*args)
        c.start()
        sent.append(c)
        return c

    def embed(resid, hidden, weight, emb_out, dir_out, len_out):
        edge = dot(hidden[...], weight[...]) + resid[:, BLK:].astype(F32)
        body = resid[:, :BLK].astype(F32)
        square = jnp.sum(body * body, axis=1, keepdims=True) + jnp.sum(
            edge * edge, axis=1, keepdims=True
        )
        length = jnp.sqrt(square + 1e-06)
        inverse = 1.0 / length
        emb_out[:, :BLK] = (body * inverse).astype(BF16)
        direction = edge * inverse
        emb_out[:, BLK:] = direction.astype(BF16)
        dir_out[...] = direction
        len_out[...] = jnp.broadcast_to(inverse, len_out.shape)

    for n in range(3):
        loads[n].wait()
    embed(tr, th, ew.at[1], temb, tdir, tlen)
    pl.semaphore_wait(barrier, len(peers))

    far = [
        remote(temb.at[part], vis.at[1, part], vs_sem.at[n + 1], vr_sem.at[n + 1], along(2))
        for n, part in enumerate((pl.ds(0, 64), pl.ds(64, 64)))
    ]
    near_copy = remote(temb, vis.at[0], vs_sem.at[0], vr_sem.at[0], cpeer)
    onward = remote(vis.at[1], vis.at[0], vs_sem.at[0], vr_sem.at[0], cpeer)

    @pl.when(core == 1)
    def _():
        far[0].start()
        far[1].start()

    @pl.when(core == 0)
    def _():
        near_copy.start()

    for d in near:
        pl.semaphore_signal(ready, inc=1, device_id=d, device_id_type=MESH)
    for c in loads[6:]:
        c.start()
    for n in range(3, 6):
        loads[n].wait()
    embed(ir, ih, ew.at[0], emb.at[half_rows], idir, ilen)
    send(emb.at[half_rows], emb.at[half_rows], es_sem, er_sem, opeer)

    iht[...] = ih[...].T
    tht[...] = th[...].T

    @pl.when(core == 1)
    def _():
        far[0].wait_send()
        pl.semaphore_signal(go, inc=1, device_id=cpeer, device_id_type=MESH)

    @pl.when(core == 0)
    def _():
        pl.semaphore_wait(go, 1)
        far[0].start()
        far[1].start()

    def pair(view, diagonal):
        texts = view[...]
        sims = dot(emb[...], texts, (1, 1))
        probs = 1.0 / (1.0 + jnp.exp(2.0 - 10.0 * sims))
        if diagonal:
            image = lax.broadcasted_iota(jnp.int32, sims.shape, 0)
            text = lax.broadcasted_iota(jnp.int32, sims.shape, 1) + xl * ROWS
            probs = probs - (text == image).astype(F32)
        weights = probs.astype(BF16)
        radial = weights.astype(F32) * sims
        img_edge = dot(weights, texts[:, BLK:])
        img_radial = jnp.sum(radial, axis=1, keepdims=True)
        txt_edge = dot(weights, emb[:, BLK:], (0, 0))
        txt_radial = jnp.sum(radial, axis=0, keepdims=True)
        return txt_edge, txt_radial, img_edge, jnp.broadcast_to(img_radial, (TXT, EDGE))

    @pl.when(core == 1)
    def _():
        far[0].wait_recv()
        far[1].wait_recv()
        onward.start()

    remote(emb.at[other_rows], emb.at[other_rows], es_sem, er_sem, opeer).wait_recv()
    own_edge, own_radial, img_edge, img_radial = pair(temb, True)
    back[2, :ROWS] = own_edge
    back[2, ROWS:] = jnp.broadcast_to(own_radial, (8, EDGE))
    iedge[...] = img_edge
    iradial[...] = img_radial

    for slot in range(2):
        if slot == 0:
            near_copy.wait_recv()
        else:
            @pl.when(core == 0)
            def _():
                far[0].wait_recv()
                far[1].wait_recv()

        edge, radial, img_edge, img_radial = pair(vis.at[slot], False)
        back[slot, :ROWS] = edge
        back[slot, ROWS:] = jnp.broadcast_to(radial, (8, EDGE))
        send(back.at[slot], back_in.at[slot], bs_sem.at[slot], br_sem.at[slot], before[slot])
        iedge[...] = iedge[...] + img_edge
        iradial[...] = iradial[...] + img_radial
    sent.append(far[1])
    sent.append(near_copy)
    tout[:ROWS] = iedge[other_rows]
    tout[ROWS:] = iradial[other_rows].T[:8]
    send(tout, tin, ts_sem, tr_sem, opeer)

    mine = rows_at(core * 512, 512)
    theirs = rows_at(oc * 512, 512)

    def edge_dz(edge, radial, direction, inverse):
        return ((edge - direction[...] * radial) * inverse[...]).astype(BF16)

    def across(row):
        return jnp.broadcast_to(row, (ROWS, EDGE)).T

    remote(tin, tin, ts_sem, tr_sem, opeer).wait_recv()
    radial = iradial[half_rows] + across(tin[ROWS:ROWS + 1])
    dz = edge_dz(iedge[half_rows] + tin[:ROWS], radial, idir, ilen)
    csend[0] = dot(iht[theirs], dz).astype(BF16)
    ccopies = [send(csend.at[0], cbuf.at[0], cs_sem.at[0], cr_sem.at[0], cpeer)]
    p[0] = dot(iht[mine], dz)
    for slot in range(2):
        remote(
            back.at[slot], back_in.at[slot], bs_sem.at[slot], br_sem.at[slot], cpeer
        ).wait_recv()
    total = back[2] + back_in[0] + back_in[1]
    dz = edge_dz(total[:ROWS], across(total[ROWS:ROWS + 1]), tdir, tlen)
    csend[1] = dot(tht[theirs], dz).astype(BF16)
    ccopies.append(send(csend.at[1], cbuf.at[1], cs_sem.at[1], cr_sem.at[1], cpeer))
    p[1] = dot(tht[mine], dz)

    pieces = [lax.rem(y + k, NY) for k in YORDER + (0,)]
    for t in range(2):
        ccopies[t].wait_recv()
        acc1[t] = (p[t] + cbuf[t].astype(F32)).reshape(NY, 2, 32, EDGE)
        for h in (1, 0):
            k = lax.rem(2 * h + t + 4 - x, 4)
            slot = lax.max(k - 1, 0)

            @pl.when(k > 0)
            def _():
                xsend[slot] = acc1[t, :, h].astype(BF16)
                for n, q in enumerate(pieces):
                    remote(
                        xsend.at[slot, q], xbuf.at[slot, q], xs_sem.at[slot, n],
                        xr_sem.at[slot, n], at(xh=h, xl=t),
                    ).start()

    loads[6].wait()

    @pl.loop(0, 8)
    def _(i):
        r = rows_at(i * 128, 128)
        value = left[r]
        high = value.astype(BF16)
        lhi[r] = high
        llo[r] = (value - high.astype(F32)).astype(BF16)

    pl.semaphore_wait(ready, len(near))
    ycopies = []
    for n, q in enumerate(pieces):
        part = acc1[xl, q, xh]
        for k in range(3):
            c = remote(
                xsend.at[k, q], xbuf.at[k, q], xs_sem.at[k, n], xr_sem.at[k, n], cpeer
            )
            c.wait_recv()
            sent.append(c)
            part = part + xbuf[k, q].astype(F32)
        if n < NY - 1:
            ysend[q] = part.astype(BF16)
            k = YORDER[n]
            ycopies.append(send(
                ysend.at[q], ybuf.at[k - 1], ys_sem.at[k - 1], yr_sem.at[k - 1], ypeer[k - 1][1]
            ))
    for c in ycopies:
        c.wait_recv()
    for k in range(NY - 1):
        part = part + ybuf[k].astype(F32)
    zbuf[z] = part.astype(BF16)
    for k in ZORDER:
        send(zbuf.at[z], zbuf.at[z], zs_sem.at[k - 1], zr_sem.at[k - 1], zpeer[k - 1][1])
    loads[7].wait()
    loads[8].wait()
    value = right[...]
    high = value.astype(BF16)
    rboth = jnp.concatenate([high, (value - high.astype(F32)).astype(BF16)], axis=1)
    for k in ZORDER:
        src = lax.rem(z + NZ - k, NZ)
        remote(zbuf.at[src], zbuf.at[src], zs_sem.at[k - 1], zr_sem.at[k - 1], cpeer).wait_recv()
    part = zbuf[0].astype(F32)
    for k in range(1, NZ):
        part = part + zbuf[k].astype(F32)
    at_y = core * NY + y
    gbuf[at_y, xh] = part.astype(BF16)
    own = gbuf.at[at_y, xh]
    offsets = [(k, h) for k in (4, 3, 5, 2, 6, 1, 7, 0) for h in (1, 0)][:-1]
    for n, (k, h) in enumerate(offsets):
        d = at(y=lax.rem(y + k, NY), xh=lax.rem(xh + h, 2))
        send(own, own, gs_sem.at[n], gr_sem.at[n], d)
    for n, (k, h) in enumerate(offsets):
        came = gbuf.at[core * NY + lax.rem(y + NY - k, NY), lax.rem(xh + h, 2)]
        remote(came, came, gs_sem.at[n], gr_sem.at[n], cpeer).wait_recv()
    own = gbuf.at[pl.ds(core * NY, NY)]
    send(own, own, ks_sem, kr_sem, cpeer)

    def half(c, first):
        g = gbuf[pl.ds(c * NY, NY)].reshape(512, EDGE)
        r = rows_at(c * 512, 512)
        v = dot(g, rboth)
        v = v[:, :EDGE] + v[:, EDGE:]
        high = v.astype(BF16)
        both = jnp.concatenate([high, (v - high.astype(F32)).astype(BF16)], axis=1)

        def body(i, total):
            o = rows_at(i * 256, 256)
            v = dot(lhi[o, r], both)
            v = v[:, :EDGE] + v[:, EDGE:] + dot(llo[o, r], high)
            if not first:
                v = v + cond[o]
            cond[o] = v
            return total if first else total + jnp.sum(v * v)

        csum = lax.fori_loop(0, 4, body, jnp.float32(0.0))
        g = g.astype(F32)
        square = g * g
        return jnp.sum(square / (acc[r] + square)), csum

    gsum, _ = half(core, True)
    other = gbuf.at[pl.ds(oc * NY, NY)]
    remote(other, other, ks_sem, kr_sem, cpeer).wait_recv()
    more, csum = half(oc, False)
    factor = jnp.sqrt(gsum + more) / jnp.sqrt(csum + 1e-06)
    out_ref[...] = cond[...] * factor
    for c in sent:
        c.wait_send()

    @pl.when(core == 0)
    def _():
        far[0].wait_send()


def on_device(*args):
    dma = pltpu.SemaphoreType.DMA
    hbm = pl.BlockSpec(memory_space=pl.ANY)

    def f32(*shape):
        return pltpu.VMEM(shape, F32)

    def bf16(*shape):
        return pltpu.VMEM(shape, BF16)

    args = args[:5] + tuple(a.reshape(a.shape[1:]) for a in args[5:])
    out = pl.pallas_call(
        kernel,
        out_shape=jax.ShapeDtypeStruct((BLK, EDGE), F32),
        in_specs=[hbm] * 8,
        out_specs=pl.BlockSpec(memory_space=pltpu.VMEM),
        scratch_shapes=[
            bf16(ROWS, D), bf16(ROWS, BLK), bf16(ROWS, D), bf16(ROWS, BLK), bf16(2, BLK, EDGE),
            f32(BLK, BLK), f32(EDGE, EDGE), f32(BLK, EDGE),
            bf16(TXT, D), f32(ROWS, EDGE), f32(ROWS, EDGE),
            bf16(ROWS, D), f32(ROWS, EDGE), f32(ROWS, EDGE),
            bf16(2, ROWS, D), f32(3, ROWS + 8, EDGE), f32(2, ROWS + 8, EDGE),
            f32(TXT, EDGE), f32(TXT, EDGE), f32(ROWS + 8, EDGE), f32(ROWS + 8, EDGE),
            bf16(BLK, ROWS), bf16(BLK, ROWS),
            bf16(BLK, BLK), bf16(BLK, BLK),
            f32(2, 512, EDGE), bf16(2, 512, EDGE), bf16(2, 512, EDGE), f32(2, NY, 2, 32, EDGE),
            bf16(3, NY, 32, EDGE), bf16(3, NY, 32, EDGE),
            bf16(NY, 32, EDGE), bf16(NY - 1, 32, EDGE), bf16(NZ, 32, EDGE),
            bf16(2 * NY, 2, 32, EDGE), f32(BLK, EDGE),
            pltpu.SemaphoreType.REGULAR, pltpu.SemaphoreType.REGULAR,
            dma((9,)), dma, dma, dma((3,)), dma((3,)), dma((2,)), dma((2,)), dma, dma,
            dma((2,)), dma((2,)), dma((3, NY)), dma((3, NY)), dma((NY - 1,)), dma((NY - 1,)),
            dma((NZ - 1,)), dma((NZ - 1,)), dma((2 * NY - 1,)), dma((2 * NY - 1,)),
            dma, dma,
        ],
        compiler_params=pltpu.CompilerParams(
            collective_id=0, has_side_effects=True, vmem_limit_bytes=60 << 20
        ),
    )(*args)
    return out[None]


def solution(mesh):
    placed = (
        P(("dp", "opt"), None),
        P(("dp", "opt"), None),
        P("dp", None),
        P("dp", None),
        P(),
        P("opt", None, None),
        P("opt", None, None),
        P("opt", None, None),
    )
    return jax.shard_map(
        on_device, mesh=mesh, in_specs=placed, out_specs=P("opt", None, None), check_vma=False
    )
```

```python
import jax
import jax.numpy as jnp
from jax import lax
from jax.experimental import pallas as pl
from jax.experimental.pallas import tpu as pltpu
from jax.sharding import PartitionSpec as P

NX, NY, NZ, NDP = 2, 8, 12, 384
D, BLK, EDGE = 1152, 1024, 128
ROWS, TXT = 128, 256
MESH = pl.DeviceIdType.MESH
F32 = jnp.float32
BF16 = jnp.bfloat16
YORDER = (4, 3, 5, 2, 6, 1, 7)
ZORDER = (6, 5, 7, 4, 8, 3, 9, 2, 10, 1, 11)


def rows_at(start, size):
    return pl.ds(pl.multiple_of(start, size), size)


def dot(a, b, dims=(1, 0)):
    return lax.dot_general(
        a, b, (((dims[0],), (dims[1],)), ((), ())), preferred_element_type=F32
    )


def kernel(
    img_resid, img_hidden, txt_resid, txt_hidden, edge_weight, left_hbm, right_hbm, acc_hbm,
    out_ref,
    ir, ih, tr, th, ew, left, right, acc,
    emb, idir, ilen, temb, tdir, tlen, vis, back, back_in, iedge, iradial, tout, tin,
    iht, tht, lhi, llo,
    p, csend, cbuf, acc1, xsend, xbuf, ysend, ybuf, zbuf, gbuf, cond, ready, go,
    load_sem, es_sem, er_sem, vs_sem, vr_sem, bs_sem, br_sem, ts_sem, tr_sem,
    cs_sem, cr_sem, xs_sem, xr_sem, ys_sem, yr_sem, zs_sem, zr_sem,
    gs_sem, gr_sem, ks_sem, kr_sem,
):
    dp = lax.axis_index("dp")
    xl = lax.axis_index("opt")
    core = lax.rem(dp, 2)
    y = lax.rem(lax.div(dp, 2), NY)
    z = lax.rem(lax.div(dp, 2 * NY), NZ)
    xh = lax.div(dp, 2 * NY * NZ)
    oc = 1 - core

    def at(xh=xh, z=z, y=y, core=core, xl=xl):
        return (((xh * NZ + z) * NY + y) * 2 + core, xl)

    half_rows = rows_at(xl * ROWS, ROWS)
    other_rows = rows_at((1 - xl) * ROWS, ROWS)
    loads = []
    for n, (src, dst) in enumerate([
        (txt_hidden.at[half_rows], th), (edge_weight.at[1], ew.at[1]),
        (txt_resid.at[half_rows], tr),
        (img_hidden, ih), (edge_weight.at[0], ew.at[0]), (img_resid, ir),
        (left_hbm, left), (right_hbm, right), (acc_hbm, acc),
    ]):
        loads.append(pltpu.make_async_copy(src, dst, load_sem.at[n]))
    for c in loads[:3]:
        c.start()

    x = xh * 2 + xl
    xpeer = []
    for k in range(1, 4):
        px = lax.rem(x + k, 4)
        xpeer.append((px, at(xh=lax.div(px, 2), xl=lax.rem(px, 2))))
    ypeer = [(lax.rem(y + k, NY), at(y=lax.rem(y + k, NY))) for k in range(1, NY)]
    zpeer = [(lax.rem(z + k, NZ), at(z=lax.rem(z + k, NZ))) for k in range(1, NZ)]
    cpeer = at(core=oc)
    opeer = (dp, 1 - xl)

    def along(c):
        there = lax.rem(dp + NDP + c, NDP)
        return there, lax.rem(xl + xh + lax.div(there, 2 * NY * NZ), 2)

    before = [along(-1), along(-2)]
    side = along(2 * core - 1)

    barrier = pltpu.get_barrier_semaphore()
    one = [xpeer[0][1], xpeer[2][1]] + [ypeer[k - 1][1] for k in (1, 7)] + [
        zpeer[k - 1][1] for k in (1, 11)
    ]
    z_two = [zpeer[k - 1][1] for k in (2, 10)]
    two = [ypeer[k - 1][1] for k in (2, 6)] + z_two
    peers = [along(2), before[1], side, cpeer] + one

    def tell(sem, devices):
        for d in devices:
            pl.semaphore_signal(sem, inc=1, device_id=d, device_id_type=MESH)

    tell(barrier, peers)
    for c in loads[3:6]:
        c.start()

    def remote(src, dst, s, r, d):
        return pltpu.make_async_remote_copy(
            src_ref=src, dst_ref=dst, send_sem=s, recv_sem=r, device_id=d, device_id_type=MESH
        )

    sent = []

    def send(*args):
        c = remote(*args)
        c.start()
        sent.append(c)
        return c

    def embed(resid, hidden, weight, emb_out, dir_out, len_out):
        edge = dot(hidden[...], weight[...]) + resid[:, BLK:].astype(F32)
        body = resid[:, :BLK].astype(F32)
        square = jnp.sum(body * body, axis=1, keepdims=True) + jnp.sum(
            edge * edge, axis=1, keepdims=True
        )
        length = jnp.sqrt(square + 1e-06)
        inverse = 1.0 / length
        emb_out[:, :BLK] = (body * inverse).astype(BF16)
        direction = edge * inverse
        emb_out[:, BLK:] = direction.astype(BF16)
        dir_out[...] = direction
        len_out[...] = jnp.broadcast_to(inverse, len_out.shape)

    for n in range(3):
        loads[n].wait()
    embed(tr, th, ew.at[1], temb, tdir, tlen)
    pl.semaphore_wait(barrier, len(peers))

    far = [
        remote(temb.at[part], vis.at[1, part], vs_sem.at[n + 1], vr_sem.at[n + 1], along(2))
        for n, part in enumerate((pl.ds(0, 64), pl.ds(64, 64)))
    ]
    near_copy = remote(temb, vis.at[0], vs_sem.at[0], vr_sem.at[0], cpeer)
    onward = remote(vis.at[1], vis.at[0], vs_sem.at[0], vr_sem.at[0], cpeer)

    @pl.when(core == 1)
    def _():
        far[0].start()
        far[1].start()

    @pl.when(core == 0)
    def _():
        near_copy.start()

    tell(ready.at[0], one)
    for c in loads[6:]:
        c.start()
    for n in range(3, 6):
        loads[n].wait()
    embed(ir, ih, ew.at[0], emb.at[half_rows], idir, ilen)
    send(emb.at[half_rows], emb.at[half_rows], es_sem, er_sem, opeer)

    iht[...] = ih[...].T
    tht[...] = th[...].T

    @pl.when(core == 1)
    def _():
        far[0].wait_send()
        pl.semaphore_signal(go, inc=1, device_id=cpeer, device_id_type=MESH)

    @pl.when(core == 0)
    def _():
        pl.semaphore_wait(go, 1)
        far[0].start()
        far[1].start()

    def pair(view, diagonal):
        texts = view[...]
        sims = dot(emb[...], texts, (1, 1))
        probs = 1.0 / (1.0 + jnp.exp(2.0 - 10.0 * sims))
        if diagonal:
            image = lax.broadcasted_iota(jnp.int32, sims.shape, 0)
            text = lax.broadcasted_iota(jnp.int32, sims.shape, 1) + xl * ROWS
            probs = probs - (text == image).astype(F32)
        weights = probs.astype(BF16)
        radial = weights.astype(F32) * sims
        img_edge = dot(weights, texts[:, BLK:])
        img_radial = jnp.sum(radial, axis=1, keepdims=True)
        txt_edge = dot(weights, emb[:, BLK:], (0, 0))
        txt_radial = jnp.sum(radial, axis=0, keepdims=True)
        return txt_edge, txt_radial, img_edge, jnp.broadcast_to(img_radial, (TXT, EDGE))

    @pl.when(core == 1)
    def _():
        far[0].wait_recv()
        far[1].wait_recv()
        onward.start()

    pl.semaphore_wait(ready.at[0], len(one))
    tell(ready.at[1], two)
    remote(emb.at[other_rows], emb.at[other_rows], es_sem, er_sem, opeer).wait_recv()
    own_edge, own_radial, img_edge, img_radial = pair(temb, True)
    back[2, :ROWS] = own_edge
    back[2, ROWS:] = jnp.broadcast_to(own_radial, (8, EDGE))
    iedge[...] = img_edge
    iradial[...] = img_radial

    pl.semaphore_wait(ready.at[1], len(two))
    tell(ready.at[2], z_two)

    for slot in range(2):
        if slot == 0:
            near_copy.wait_recv()
        else:
            @pl.when(core == 0)
            def _():
                far[0].wait_recv()
                far[1].wait_recv()

        edge, radial, img_edge, img_radial = pair(vis.at[slot], False)
        back[slot, :ROWS] = edge
        back[slot, ROWS:] = jnp.broadcast_to(radial, (8, EDGE))
        send(back.at[slot], back_in.at[slot], bs_sem.at[slot], br_sem.at[slot], before[slot])
        iedge[...] = iedge[...] + img_edge
        iradial[...] = iradial[...] + img_radial
    sent.append(far[1])
    sent.append(near_copy)
    tout[:ROWS] = iedge[other_rows]
    tout[ROWS:] = iradial[other_rows].T[:8]
    send(tout, tin, ts_sem, tr_sem, opeer)

    mine = rows_at(core * 512, 512)
    theirs = rows_at(oc * 512, 512)

    def edge_dz(edge, radial, direction, inverse):
        return ((edge - direction[...] * radial) * inverse[...]).astype(BF16)

    def across(row):
        return jnp.broadcast_to(row, (ROWS, EDGE)).T

    remote(tin, tin, ts_sem, tr_sem, opeer).wait_recv()
    radial = iradial[half_rows] + across(tin[ROWS:ROWS + 1])
    dz = edge_dz(iedge[half_rows] + tin[:ROWS], radial, idir, ilen)
    csend[0] = dot(iht[theirs], dz).astype(BF16)
    ccopies = [send(csend.at[0], cbuf.at[0], cs_sem.at[0], cr_sem.at[0], cpeer)]
    p[0] = dot(iht[mine], dz)
    for slot in range(2):
        remote(
            back.at[slot], back_in.at[slot], bs_sem.at[slot], br_sem.at[slot], cpeer
        ).wait_recv()
    total = back[2] + back_in[0] + back_in[1]
    dz = edge_dz(total[:ROWS], across(total[ROWS:ROWS + 1]), tdir, tlen)
    csend[1] = dot(tht[theirs], dz).astype(BF16)
    ccopies.append(send(csend.at[1], cbuf.at[1], cs_sem.at[1], cr_sem.at[1], cpeer))
    p[1] = dot(tht[mine], dz)

    pieces = [lax.rem(y + k, NY) for k in YORDER + (0,)]
    for t in range(2):
        ccopies[t].wait_recv()
        acc1[t] = (p[t] + cbuf[t].astype(F32)).reshape(NY, 2, 32, EDGE)
        for h in (1, 0):
            k = lax.rem(2 * h + t + 4 - x, 4)
            slot = lax.max(k - 1, 0)

            @pl.when(k > 0)
            def _():
                xsend[slot] = acc1[t, :, h].astype(BF16)
                for n, q in enumerate(pieces):
                    remote(
                        xsend.at[slot, q], xbuf.at[slot, q], xs_sem.at[slot, n],
                        xr_sem.at[slot, n], at(xh=h, xl=t),
                    ).start()

    loads[6].wait()

    @pl.loop(0, 8)
    def _(i):
        r = rows_at(i * 128, 128)
        value = left[r]
        high = value.astype(BF16)
        lhi[r] = high
        llo[r] = (value - high.astype(F32)).astype(BF16)

    pl.semaphore_wait(ready.at[2], len(z_two))
    ycopies = []
    for n, q in enumerate(pieces):
        part = acc1[xl, q, xh]
        for k in range(3):
            c = remote(
                xsend.at[k, q], xbuf.at[k, q], xs_sem.at[k, n], xr_sem.at[k, n], cpeer
            )
            c.wait_recv()
            sent.append(c)
            part = part + xbuf[k, q].astype(F32)
        if n < NY - 1:
            ysend[q] = part.astype(BF16)
            k = YORDER[n]
            ycopies.append(send(
                ysend.at[q], ybuf.at[k - 1], ys_sem.at[k - 1], yr_sem.at[k - 1], ypeer[k - 1][1]
            ))
    for c in ycopies:
        c.wait_recv()
    for k in range(NY - 1):
        part = part + ybuf[k].astype(F32)
    zbuf[z] = part.astype(BF16)
    for k in ZORDER:
        send(zbuf.at[z], zbuf.at[z], zs_sem.at[k - 1], zr_sem.at[k - 1], zpeer[k - 1][1])
    loads[7].wait()
    loads[8].wait()
    value = right[...]
    high = value.astype(BF16)
    rboth = jnp.concatenate([high, (value - high.astype(F32)).astype(BF16)], axis=1)
    for k in ZORDER:
        src = lax.rem(z + NZ - k, NZ)
        remote(zbuf.at[src], zbuf.at[src], zs_sem.at[k - 1], zr_sem.at[k - 1], cpeer).wait_recv()
    part = zbuf[0].astype(F32)
    for k in range(1, NZ):
        part = part + zbuf[k].astype(F32)
    at_y = core * NY + y
    gbuf[at_y, xh] = part.astype(BF16)
    own = gbuf.at[at_y, xh]
    offsets = [(k, h) for k in (4, 3, 5, 2, 6, 1, 7, 0) for h in (1, 0)][:-1]
    for n, (k, h) in enumerate(offsets):
        d = at(y=lax.rem(y + k, NY), xh=lax.rem(xh + h, 2))
        send(own, own, gs_sem.at[n], gr_sem.at[n], d)
    for n, (k, h) in enumerate(offsets):
        came = gbuf.at[core * NY + lax.rem(y + NY - k, NY), lax.rem(xh + h, 2)]
        remote(came, came, gs_sem.at[n], gr_sem.at[n], cpeer).wait_recv()
    own = gbuf.at[pl.ds(core * NY, NY)]
    send(own, own, ks_sem, kr_sem, cpeer)

    def half(c, first):
        g = gbuf[pl.ds(c * NY, NY)].reshape(512, EDGE)
        r = rows_at(c * 512, 512)
        v = dot(g, rboth)
        v = v[:, :EDGE] + v[:, EDGE:]
        high = v.astype(BF16)
        both = jnp.concatenate([high, (v - high.astype(F32)).astype(BF16)], axis=1)

        def body(i, total):
            o = rows_at(i * 256, 256)
            v = dot(lhi[o, r], both)
            v = v[:, :EDGE] + v[:, EDGE:] + dot(llo[o, r], high)
            if not first:
                v = v + cond[o]
            cond[o] = v
            return total if first else total + jnp.sum(v * v)

        csum = lax.fori_loop(0, 4, body, jnp.float32(0.0))
        g = g.astype(F32)
        square = g * g
        return jnp.sum(square / (acc[r] + square)), csum

    gsum, _ = half(core, True)
    other = gbuf.at[pl.ds(oc * NY, NY)]
    remote(other, other, ks_sem, kr_sem, cpeer).wait_recv()
    more, csum = half(oc, False)
    factor = jnp.sqrt(gsum + more) / jnp.sqrt(csum + 1e-06)
    out_ref[...] = cond[...] * factor
    for c in sent:
        c.wait_send()

    @pl.when(core == 0)
    def _():
        far[0].wait_send()


def on_device(*args):
    dma = pltpu.SemaphoreType.DMA
    hbm = pl.BlockSpec(memory_space=pl.ANY)

    def f32(*shape):
        return pltpu.VMEM(shape, F32)

    def bf16(*shape):
        return pltpu.VMEM(shape, BF16)

    args = args[:5] + tuple(a.reshape(a.shape[1:]) for a in args[5:])
    out = pl.pallas_call(
        kernel,
        out_shape=jax.ShapeDtypeStruct((BLK, EDGE), F32),
        in_specs=[hbm] * 8,
        out_specs=pl.BlockSpec(memory_space=pltpu.VMEM),
        scratch_shapes=[
            bf16(ROWS, D), bf16(ROWS, BLK), bf16(ROWS, D), bf16(ROWS, BLK), bf16(2, BLK, EDGE),
            f32(BLK, BLK), f32(EDGE, EDGE), f32(BLK, EDGE),
            bf16(TXT, D), f32(ROWS, EDGE), f32(ROWS, EDGE),
            bf16(ROWS, D), f32(ROWS, EDGE), f32(ROWS, EDGE),
            bf16(2, ROWS, D), f32(3, ROWS + 8, EDGE), f32(2, ROWS + 8, EDGE),
            f32(TXT, EDGE), f32(TXT, EDGE), f32(ROWS + 8, EDGE), f32(ROWS + 8, EDGE),
            bf16(BLK, ROWS), bf16(BLK, ROWS),
            bf16(BLK, BLK), bf16(BLK, BLK),
            f32(2, 512, EDGE), bf16(2, 512, EDGE), bf16(2, 512, EDGE), f32(2, NY, 2, 32, EDGE),
            bf16(3, NY, 32, EDGE), bf16(3, NY, 32, EDGE),
            bf16(NY, 32, EDGE), bf16(NY - 1, 32, EDGE), bf16(NZ, 32, EDGE),
            bf16(2 * NY, 2, 32, EDGE), f32(BLK, EDGE),
            pltpu.SemaphoreType.REGULAR((3,)), pltpu.SemaphoreType.REGULAR,
            dma((9,)), dma, dma, dma((3,)), dma((3,)), dma((2,)), dma((2,)), dma, dma,
            dma((2,)), dma((2,)), dma((3, NY)), dma((3, NY)), dma((NY - 1,)), dma((NY - 1,)),
            dma((NZ - 1,)), dma((NZ - 1,)), dma((2 * NY - 1,)), dma((2 * NY - 1,)),
            dma, dma,
        ],
        compiler_params=pltpu.CompilerParams(
            collective_id=0, has_side_effects=True, vmem_limit_bytes=60 << 20
        ),
    )(*args)
    return out[None]


def solution(mesh):
    placed = (
        P(("dp", "opt"), None),
        P(("dp", "opt"), None),
        P("dp", None),
        P("dp", None),
        P(),
        P("opt", None, None),
        P("opt", None, None),
        P("opt", None, None),
    )
    return jax.shard_map(
        on_device, mesh=mesh, in_specs=placed, out_specs=P("opt", None, None), check_vma=False
    )
```

```python
import jax
import jax.numpy as jnp
from jax import lax
from jax.experimental import pallas as pl
from jax.experimental.pallas import tpu as pltpu
from jax.sharding import PartitionSpec as P

NX, NY, NZ, NDP = 2, 8, 12, 384
D, BLK, EDGE = 1152, 1024, 128
ROWS, TXT = 128, 256
MESH = pl.DeviceIdType.MESH
F32 = jnp.float32
BF16 = jnp.bfloat16
YORDER = (4, 3, 5, 2, 6, 1, 7)
ZORDER = (6, 5, 7, 4, 8, 3, 9, 2, 10, 1, 11)


def rows_at(start, size):
    return pl.ds(pl.multiple_of(start, size), size)


def dot(a, b, dims=(1, 0)):
    return lax.dot_general(
        a, b, (((dims[0],), (dims[1],)), ((), ())), preferred_element_type=F32
    )


def kernel(
    img_resid, img_hidden, txt_resid, txt_hidden, edge_weight, left_hbm, right_hbm, acc_hbm,
    out_ref,
    ir, ih, tr, th, ew, left, right, acc,
    emb, idir, ilen, temb, tdir, tlen, vis, back, back_in, iedge, iradial, tout, tin,
    iht, tht, lhi, llo,
    p, csend, cbuf, acc1, xsend, xbuf, ysend, ybuf, zbuf, gbuf, cond, ready, go,
    load_sem, es_sem, er_sem, vs_sem, vr_sem, bs_sem, br_sem, ts_sem, tr_sem,
    cs_sem, cr_sem, xs_sem, xr_sem, ys_sem, yr_sem, zs_sem, zr_sem,
    gs_sem, gr_sem, ks_sem, kr_sem,
):
    dp = lax.axis_index("dp")
    xl = lax.axis_index("opt")
    core = lax.rem(dp, 2)
    y = lax.rem(lax.div(dp, 2), NY)
    z = lax.rem(lax.div(dp, 2 * NY), NZ)
    xh = lax.div(dp, 2 * NY * NZ)
    oc = 1 - core

    def at(xh=xh, z=z, y=y, core=core, xl=xl):
        return (((xh * NZ + z) * NY + y) * 2 + core, xl)

    half_rows = rows_at(xl * ROWS, ROWS)
    other_rows = rows_at((1 - xl) * ROWS, ROWS)
    loads = []
    for n, (src, dst) in enumerate([
        (txt_hidden.at[half_rows], th), (edge_weight.at[1], ew.at[1]),
        (txt_resid.at[half_rows], tr),
        (img_hidden, ih), (edge_weight.at[0], ew.at[0]), (img_resid, ir),
        (left_hbm, left), (right_hbm, right), (acc_hbm, acc),
    ]):
        loads.append(pltpu.make_async_copy(src, dst, load_sem.at[n]))
    for c in loads[:3]:
        c.start()

    x = xh * 2 + xl
    xpeer = []
    for k in range(1, 4):
        px = lax.rem(x + k, 4)
        xpeer.append((px, at(xh=lax.div(px, 2), xl=lax.rem(px, 2))))
    ypeer = [(lax.rem(y + k, NY), at(y=lax.rem(y + k, NY))) for k in range(1, NY)]
    zpeer = [(lax.rem(z + k, NZ), at(z=lax.rem(z + k, NZ))) for k in range(1, NZ)]
    cpeer = at(core=oc)
    opeer = (dp, 1 - xl)

    def along(c):
        there = lax.rem(dp + NDP + c, NDP)
        return there, lax.rem(xl + xh + lax.div(there, 2 * NY * NZ), 2)

    before = [along(-1), along(-2)]
    side = along(2 * core - 1)

    barrier = pltpu.get_barrier_semaphore()
    one = [xpeer[0][1], xpeer[2][1]] + [ypeer[k - 1][1] for k in (1, 7)] + [
        zpeer[k - 1][1] for k in (1, 11)
    ]
    z_two = [zpeer[k - 1][1] for k in (2, 10)]
    two = [ypeer[k - 1][1] for k in (2, 6)] + z_two
    peers = [along(2), before[1], side, cpeer] + one

    def tell(sem, devices):
        for d in devices:
            pl.semaphore_signal(sem, inc=1, device_id=d, device_id_type=MESH)

    tell(barrier, peers)
    for c in loads[3:6]:
        c.start()

    def remote(src, dst, s, r, d):
        return pltpu.make_async_remote_copy(
            src_ref=src, dst_ref=dst, send_sem=s, recv_sem=r, device_id=d, device_id_type=MESH
        )

    sent = []

    def send(*args):
        c = remote(*args)
        c.start()
        sent.append(c)
        return c

    def embed(resid, hidden, weight, emb_out, dir_out, len_out):
        edge = dot(hidden[...], weight[...]) + resid[:, BLK:].astype(F32)
        body = resid[:, :BLK].astype(F32)
        square = jnp.sum(body * body, axis=1, keepdims=True) + jnp.sum(
            edge * edge, axis=1, keepdims=True
        )
        length = jnp.sqrt(square + 1e-06)
        inverse = 1.0 / length
        emb_out[:, :BLK] = (body * inverse).astype(BF16)
        direction = edge * inverse
        emb_out[:, BLK:] = direction.astype(BF16)
        dir_out[...] = direction
        len_out[...] = jnp.broadcast_to(inverse, len_out.shape)

    for n in range(3):
        loads[n].wait()
    embed(tr, th, ew.at[1], temb, tdir, tlen)
    pl.semaphore_wait(barrier, len(peers))

    far = [
        remote(temb.at[part], vis.at[1, part], vs_sem.at[n + 1], vr_sem.at[n + 1], along(2))
        for n, part in enumerate((pl.ds(0, 64), pl.ds(64, 64)))
    ]
    near_copy = remote(temb, vis.at[0], vs_sem.at[0], vr_sem.at[0], cpeer)
    onward = remote(vis.at[1], vis.at[0], vs_sem.at[0], vr_sem.at[0], cpeer)

    @pl.when(core == 1)
    def _():
        far[0].start()
        far[1].start()

    @pl.when(core == 0)
    def _():
        near_copy.start()

    tell(ready.at[0], one)
    for c in loads[6:]:
        c.start()
    for n in range(3, 6):
        loads[n].wait()
    embed(ir, ih, ew.at[0], emb.at[half_rows], idir, ilen)
    send(emb.at[half_rows], emb.at[half_rows], es_sem, er_sem, opeer)

    iht[...] = ih[...].T
    tht[...] = th[...].T

    @pl.when(core == 1)
    def _():
        far[0].wait_send()
        pl.semaphore_signal(go, inc=1, device_id=cpeer, device_id_type=MESH)

    @pl.when(core == 0)
    def _():
        pl.semaphore_wait(go, 1)
        far[0].start()
        far[1].start()

    def pair(view, diagonal):
        texts = view[...]
        sims = dot(emb[...], texts, (1, 1))
        probs = 1.0 / (1.0 + jnp.exp(2.0 - 10.0 * sims))
        if diagonal:
            image = lax.broadcasted_iota(jnp.int32, sims.shape, 0)
            text = lax.broadcasted_iota(jnp.int32, sims.shape, 1) + xl * ROWS
            probs = probs - (text == image).astype(F32)
        weights = probs.astype(BF16)
        radial = weights.astype(F32) * sims
        img_edge = dot(weights, texts[:, BLK:])
        img_radial = jnp.sum(radial, axis=1, keepdims=True)
        txt_edge = dot(weights, emb[:, BLK:], (0, 0))
        txt_radial = jnp.sum(radial, axis=0, keepdims=True)
        return txt_edge, txt_radial, img_edge, jnp.broadcast_to(img_radial, (TXT, EDGE))

    @pl.when(core == 1)
    def _():
        far[0].wait_recv()
        far[1].wait_recv()
        onward.start()

    pl.semaphore_wait(ready.at[0], len(one))
    tell(ready.at[1], two)
    remote(emb.at[other_rows], emb.at[other_rows], es_sem, er_sem, opeer).wait_recv()
    own_edge, own_radial, img_edge, img_radial = pair(temb, True)
    back[2, :ROWS] = own_edge
    back[2, ROWS:] = jnp.broadcast_to(own_radial, (8, EDGE))
    iedge[...] = img_edge
    iradial[...] = img_radial

    pl.semaphore_wait(ready.at[1], len(two))
    tell(ready.at[2], z_two)

    for slot in range(2):
        if slot == 0:
            near_copy.wait_recv()
        else:
            @pl.when(core == 0)
            def _():
                far[0].wait_recv()
                far[1].wait_recv()

        edge, radial, img_edge, img_radial = pair(vis.at[slot], False)
        back[slot, :ROWS] = edge
        back[slot, ROWS:] = jnp.broadcast_to(radial, (8, EDGE))
        send(back.at[slot], back_in.at[slot], bs_sem.at[slot], br_sem.at[slot], before[slot])
        iedge[...] = iedge[...] + img_edge
        iradial[...] = iradial[...] + img_radial
    sent.append(far[1])
    sent.append(near_copy)
    tout[:ROWS] = iedge[other_rows]
    tout[ROWS:] = iradial[other_rows].T[:8]
    send(tout, tin, ts_sem, tr_sem, opeer)

    mine = rows_at(core * 512, 512)
    theirs = rows_at(oc * 512, 512)

    def edge_dz(edge, radial, direction, inverse):
        return ((edge - direction[...] * radial) * inverse[...]).astype(BF16)

    def across(row):
        return jnp.broadcast_to(row, (ROWS, EDGE)).T

    remote(tin, tin, ts_sem, tr_sem, opeer).wait_recv()
    radial = iradial[half_rows] + across(tin[ROWS:ROWS + 1])
    dz = edge_dz(iedge[half_rows] + tin[:ROWS], radial, idir, ilen)
    csend[0] = dot(iht[theirs], dz).astype(BF16)
    ccopies = [send(csend.at[0], cbuf.at[0], cs_sem.at[0], cr_sem.at[0], cpeer)]
    p[0] = dot(iht[mine], dz)
    for slot in range(2):
        remote(
            back.at[slot], back_in.at[slot], bs_sem.at[slot], br_sem.at[slot], cpeer
        ).wait_recv()
    total = back[2] + back_in[0] + back_in[1]
    dz = edge_dz(total[:ROWS], across(total[ROWS:ROWS + 1]), tdir, tlen)
    csend[1] = dot(tht[theirs], dz).astype(BF16)
    ccopies.append(send(csend.at[1], cbuf.at[1], cs_sem.at[1], cr_sem.at[1], cpeer))
    p[1] = dot(tht[mine], dz)

    pieces = [lax.rem(y + k, NY) for k in YORDER + (0,)]
    for t in range(2):
        ccopies[t].wait_recv()
        acc1[t] = (p[t] + cbuf[t].astype(F32)).reshape(NY, 2, 32, EDGE)
        for h in (1, 0):
            k = lax.rem(2 * h + t + 4 - x, 4)
            slot = lax.max(k - 1, 0)

            @pl.when(k > 0)
            def _():
                xsend[slot] = acc1[t, :, h].astype(BF16)
                for n, q in enumerate(pieces):
                    remote(
                        xsend.at[slot, q], xbuf.at[slot, q], xs_sem.at[slot, n],
                        xr_sem.at[slot, n], at(xh=h, xl=t),
                    ).start()

    loads[6].wait()

    @pl.loop(0, 8)
    def _(i):
        r = rows_at(i * 128, 128)
        value = left[r]
        high = value.astype(BF16)
        lhi[r] = high
        llo[r] = (value - high.astype(F32)).astype(BF16)

    pl.semaphore_wait(ready.at[2], len(z_two))
    ycopies = []
    for n, q in enumerate(pieces):
        part = acc1[xl, q, xh]
        for k in range(3):
            c = remote(
                xsend.at[k, q], xbuf.at[k, q], xs_sem.at[k, n], xr_sem.at[k, n], cpeer
            )
            c.wait_recv()
            sent.append(c)
            part = part + xbuf[k, q].astype(F32)
        if n < NY - 1:
            ysend[q] = part.astype(BF16)
            k = YORDER[n]
            ycopies.append(send(
                ysend.at[q], ybuf.at[k - 1], ys_sem.at[k - 1], yr_sem.at[k - 1], ypeer[k - 1][1]
            ))
    for c in ycopies:
        c.wait_recv()
    for k in range(NY - 1):
        part = part + ybuf[k].astype(F32)
    zbuf[z] = part.astype(BF16)
    for k in ZORDER:
        send(zbuf.at[z], zbuf.at[z], zs_sem.at[k - 1], zr_sem.at[k - 1], zpeer[k - 1][1])
    loads[7].wait()
    loads[8].wait()
    value = right[...]
    high = value.astype(BF16)
    rboth = jnp.concatenate([high, (value - high.astype(F32)).astype(BF16)], axis=1)
    for k in ZORDER:
        src = lax.rem(z + NZ - k, NZ)
        remote(zbuf.at[src], zbuf.at[src], zs_sem.at[k - 1], zr_sem.at[k - 1], cpeer).wait_recv()
    part = zbuf[0].astype(F32)
    for k in range(1, NZ):
        part = part + zbuf[k].astype(F32)
    at_y = core * NY + y
    gbuf[at_y, xh] = part.astype(BF16)
    own = gbuf.at[at_y, xh]
    offsets = [(k, h) for k in (4, 3, 5, 2, 6, 1, 7, 0) for h in (1, 0)][:-1]
    for n, (k, h) in enumerate(offsets):
        d = at(y=lax.rem(y + k, NY), xh=lax.rem(xh + h, 2))
        send(own, own, gs_sem.at[n], gr_sem.at[n], d)
    early = len(sent) - len(offsets)
    for c in sent[:early]:
        c.wait_send()

    @pl.when(core == 0)
    def _():
        far[0].wait_send()

    for n, (k, h) in enumerate(offsets):
        came = gbuf.at[core * NY + lax.rem(y + NY - k, NY), lax.rem(xh + h, 2)]
        remote(came, came, gs_sem.at[n], gr_sem.at[n], cpeer).wait_recv()
    own = gbuf.at[pl.ds(core * NY, NY)]
    send(own, own, ks_sem, kr_sem, cpeer)

    def half(c, first):
        g = gbuf[pl.ds(c * NY, NY)].reshape(512, EDGE)
        r = rows_at(c * 512, 512)
        v = dot(g, rboth)
        v = v[:, :EDGE] + v[:, EDGE:]
        high = v.astype(BF16)
        both = jnp.concatenate([high, (v - high.astype(F32)).astype(BF16)], axis=1)

        def body(i, total):
            o = rows_at(i * 256, 256)
            v = dot(lhi[o, r], both)
            v = v[:, :EDGE] + v[:, EDGE:] + dot(llo[o, r], high)
            if not first:
                v = v + cond[o]
            cond[o] = v
            return total if first else total + jnp.sum(v * v)

        csum = lax.fori_loop(0, 4, body, jnp.float32(0.0))
        g = g.astype(F32)
        square = g * g
        return jnp.sum(square / (acc[r] + square)), csum

    gsum, _ = half(core, True)
    other = gbuf.at[pl.ds(oc * NY, NY)]
    remote(other, other, ks_sem, kr_sem, cpeer).wait_recv()
    more, csum = half(oc, False)
    factor = jnp.sqrt(gsum + more) / jnp.sqrt(csum + 1e-06)
    out_ref[...] = cond[...] * factor
    for c in sent[early:]:
        c.wait_send()


def on_device(*args):
    dma = pltpu.SemaphoreType.DMA
    hbm = pl.BlockSpec(memory_space=pl.ANY)

    def f32(*shape):
        return pltpu.VMEM(shape, F32)

    def bf16(*shape):
        return pltpu.VMEM(shape, BF16)

    args = args[:5] + tuple(a.reshape(a.shape[1:]) for a in args[5:])
    out = pl.pallas_call(
        kernel,
        out_shape=jax.ShapeDtypeStruct((BLK, EDGE), F32),
        in_specs=[hbm] * 8,
        out_specs=pl.BlockSpec(memory_space=pltpu.VMEM),
        scratch_shapes=[
            bf16(ROWS, D), bf16(ROWS, BLK), bf16(ROWS, D), bf16(ROWS, BLK), bf16(2, BLK, EDGE),
            f32(BLK, BLK), f32(EDGE, EDGE), f32(BLK, EDGE),
            bf16(TXT, D), f32(ROWS, EDGE), f32(ROWS, EDGE),
            bf16(ROWS, D), f32(ROWS, EDGE), f32(ROWS, EDGE),
            bf16(2, ROWS, D), f32(3, ROWS + 8, EDGE), f32(2, ROWS + 8, EDGE),
            f32(TXT, EDGE), f32(TXT, EDGE), f32(ROWS + 8, EDGE), f32(ROWS + 8, EDGE),
            bf16(BLK, ROWS), bf16(BLK, ROWS),
            bf16(BLK, BLK), bf16(BLK, BLK),
            f32(2, 512, EDGE), bf16(2, 512, EDGE), bf16(2, 512, EDGE), f32(2, NY, 2, 32, EDGE),
            bf16(3, NY, 32, EDGE), bf16(3, NY, 32, EDGE),
            bf16(NY, 32, EDGE), bf16(NY - 1, 32, EDGE), bf16(NZ, 32, EDGE),
            bf16(2 * NY, 2, 32, EDGE), f32(BLK, EDGE),
            pltpu.SemaphoreType.REGULAR((3,)), pltpu.SemaphoreType.REGULAR,
            dma((9,)), dma, dma, dma((3,)), dma((3,)), dma((2,)), dma((2,)), dma, dma,
            dma((2,)), dma((2,)), dma((3, NY)), dma((3, NY)), dma((NY - 1,)), dma((NY - 1,)),
            dma((NZ - 1,)), dma((NZ - 1,)), dma((2 * NY - 1,)), dma((2 * NY - 1,)),
            dma, dma,
        ],
        compiler_params=pltpu.CompilerParams(
            collective_id=0, has_side_effects=True, vmem_limit_bytes=60 << 20
        ),
    )(*args)
    return out[None]


def solution(mesh):
    placed = (
        P(("dp", "opt"), None),
        P(("dp", "opt"), None),
        P("dp", None),
        P("dp", None),
        P(),
        P("opt", None, None),
        P("opt", None, None),
        P("opt", None, None),
    )
    return jax.shard_map(
        on_device, mesh=mesh, in_specs=placed, out_specs=P("opt", None, None), check_vma=False
    )
```
